32 devices in a mesh: tile: 8 (over z, core), member: 4 (over y, x).
Axes of the slice: x: 2, y: 2, z: 4, core: 2. Of those that a mesh axis runs over, the one named last changes fastest.
Arguments:
- coeffs: float32 [40, 32, 8192], P('member', None, 'tile'), may hold values from -6 to 6
- perturb: bfloat16 [2, 40, 32, 8192], P(None, 'member', None, 'tile'), may hold values from -2 to 2
- blocks: bfloat16 [8, 5, 1024, 1024], P('tile'), may hold values from -0.125 to 0.125
- neighbours: int32 [8, 5], P('tile'), may hold values from 0 to 7, as said below
- live: int32 [8], P('tile'), may hold values from 2 to 5, as said below
- obs_count: int32 [8], P('tile'), may hold values from 256 to 1024, as said below
- innovation: float32 [2, 32, 8192], P(None, None, 'tile'), may hold values from -6 to 6
- obs_weight: float32 [32, 8192], P(None, 'tile'), may hold values from 0.25 to 4
Outputs:
- increment: float32 [2, 32, 8192], P(None, None, ('tile', 'member'))
- gradient: float32 [40, 32, 8192], P('member', None, 'tile')
The draws below stay inside these ranges and needn't reach their ends.
Inputs may be any that keep to these rules, and one draw needn't show every extreme that they name: `neighbours`: each row lists 5 different tiles, each at a distance of at most 2 from the row's tile along the tile cycle (indices taken modulo 8); only the first live[i] slots of row i are used. Some tile has all 5 slots live. Observations of tile i lie in its first obs_count[i] columns.
All inputs are finite; a program needn't handle non-finite values.
Results may differ from the reference program's by a relative error of at most 0.0038.
Values may be sent and summed in bfloat16 or wider, within the bound.
No kernel may reach another device: no remote copies, remote signals or barrier semaphores. Data moves between devices by JAX's collectives and lax.ppermute only.
A program may use at most 64 MiB of HBM per device.

```python
import math
import jax
import jax.numpy as jnp
from jax import lax

CELL_DEV = 1024
LEV = 32
TIMES = 2
REACH = 2
KMAX = 5
TILES = 8
CELLS = 8192
MEMBERS = 40


def draw_neighbours(key, part):
    key = jax.random.fold_in(key, 11)
    tile_keys = jax.random.split(key, TILES)
    offsets = jax.vmap(lambda single: jax.random.permutation(single, KMAX))(tile_keys) - REACH
    return ((jnp.arange(TILES)[:, None] + offsets) % TILES).astype(jnp.int32)


def draw_live(key, part):
    key = jax.random.fold_in(key, 12)
    first_key, second_key = jax.random.split(key)
    counts = jax.random.randint(first_key, (TILES,), 2, KMAX + 1)
    busiest = jax.random.randint(second_key, (), 0, TILES)
    return jnp.where(jnp.arange(TILES) == busiest, KMAX, counts).astype(jnp.int32)


def draw_obs_count(key, part):
    key = jax.random.fold_in(key, 13)
    first_key, second_key = jax.random.split(key)
    counts = jax.random.randint(first_key, (TILES,), CELL_DEV // 4, CELL_DEV + 1)
    fullest = jax.random.randint(second_key, (), 0, TILES)
    tile_ids = jnp.arange(TILES)
    counts = jnp.where(tile_ids == fullest, CELL_DEV, counts)
    counts = jnp.where(tile_ids == (fullest + 1) % TILES, CELL_DEV // 4, counts)
    return counts.astype(jnp.int32)


def levels(own_key, shape, shards, smallest, high):
    def one(position, blocks):
        draws = jax.random.uniform(jax.random.fold_in(jax.random.fold_in(own_key, 6), position), (blocks,), jnp.float32, smallest / len(shards), high / len(shards))
        return jnp.repeat(jnp.exp(draws), shape[position] // blocks).reshape((-1,) + (1,) * (len(shape) - position - 1))

    loudness = one(*shards[0])
    for cut in shards[1:]:
        loudness = loudness * one(*cut)
    return loudness


def noise(own_key, extent, spread, reach, cuts=(), held_as=jnp.bfloat16):
    drawn = jax.random.normal(own_key, extent, jnp.float32) * spread
    if len(cuts) > 0:
        drawn = levels(own_key, extent, cuts, -0.22, 0.18) * drawn
    return jnp.clip(drawn, min=-reach, max=reach).astype(held_as)


def setup_inputs(seed: int = 0) -> dict:
    key_list = jax.random.split(jax.random.key(seed), 9)
    coeffs = noise(key_list[0], (MEMBERS, LEV, CELLS), 1.0, 6.0, ((0, 4), (2, 8)), jnp.float32)
    perturb = noise(key_list[1], (TIMES, MEMBERS, LEV, CELLS), (MEMBERS // 4) ** -0.5, 2.0, ((1, 4), (3, 8)))
    blocks = noise(key_list[2], (TILES, KMAX, CELL_DEV, CELL_DEV), (CELL_DEV * 2) ** -0.5, 0.125, ((0, 8),))
    neighbours = draw_neighbours(jax.random.fold_in(key_list[8], 71), 0)
    live = draw_live(jax.random.fold_in(key_list[8], 71), 0)
    obs_count = draw_obs_count(jax.random.fold_in(key_list[8], 71), 0)
    innovation = noise(key_list[6], (TIMES, LEV, CELLS), 1.0, 6.0, ((2, 8),), jnp.float32)
    obs_weight = jnp.clip(jnp.exp(math.log(4.0) - 2.7725887 * jax.random.uniform(key_list[7], (LEV, CELLS), jnp.float32) ** levels(key_list[7], (LEV, CELLS), ((1, 8),), -0.2, 0.2)), 0.25, 4.0)
    return dict(coeffs=coeffs, perturb=perturb, blocks=blocks, neighbours=neighbours, live=live, obs_count=obs_count, innovation=innovation, obs_weight=obs_weight)


def reference(coeffs, perturb, blocks, neighbours, live, obs_count, innovation, obs_weight):
    row_count = MEMBERS * LEV
    coeff_half = coeffs.astype(jnp.bfloat16).reshape(row_count, TILES, CELL_DEV)
    slot_ids = jnp.arange(KMAX)

    def forward(tile_id):
        sources = neighbours[tile_id]
        slot_live = slot_ids < live[tile_id]
        pieces = jnp.take(coeff_half, sources, axis=1).astype(jnp.float32)
        product = jnp.einsum('rkc,kcd->rkd', pieces, blocks[tile_id].astype(jnp.float32))
        return jnp.sum(jnp.where(slot_live[None, :, None], product, 0.0), axis=1)

    localized = lax.map(forward, jnp.arange(TILES))
    localized = jnp.transpose(localized, (1, 0, 2)).reshape(MEMBERS, LEV, CELLS)
    increment = jnp.sum(perturb.astype(jnp.float32) * localized[None], axis=1)
    column_ids = jnp.arange(CELLS)
    observed = (column_ids % CELL_DEV) < obs_count[column_ids // CELL_DEV]
    residual = obs_weight[None] * jnp.where(observed[None, None, :], increment - innovation, 0.0)
    adjoint_in = jnp.sum(perturb.astype(jnp.float32) * residual[:, None], axis=0)
    adjoint_in = adjoint_in.astype(jnp.bfloat16).reshape(row_count, TILES, CELL_DEV)
    tile_ids = jnp.arange(TILES)

    def backward(accum, tile_id):
        sources = neighbours[tile_id]
        slot_live = slot_ids < live[tile_id]
        local_in = lax.dynamic_index_in_dim(adjoint_in, tile_id, 1, keepdims=False).astype(jnp.float32)
        product = jnp.einsum('rd,kcd->krc', local_in, blocks[tile_id].astype(jnp.float32))
        one_hot = ((sources[:, None] == tile_ids[None, :]) & slot_live[:, None]).astype(jnp.float32)
        return accum + jnp.einsum('kt,krc->rtc', one_hot, product), None

    adjoint, unused = lax.scan(backward, jnp.zeros((row_count, TILES, CELL_DEV), jnp.float32), tile_ids)
    gradient = coeffs + adjoint.reshape(MEMBERS, LEV, CELLS)
    return increment, gradient
```

```python
import functools
import jax
import jax.numpy as jnp
from jax import lax
from jax.experimental import pallas as pl
from jax.experimental.pallas import tpu as pltpu
from jax.sharding import PartitionSpec as P

CHUNKS = 2
VMEM_LIMIT = 20 * 1024 * 1024
OWN, PARTNER, EARLY, SWAPPED, LATE = range(5)
PLACES = {"partner": PARTNER, "early": EARLY, "late": LATE}
ORDER = (0, 1, 2, -1, -2)
TURNED = (SWAPPED, LATE, EARLY)


def shift_pairs(count, step):
    return [(source, (source + step(source % 2)) % count) for source in range(count)]


def member_terms(value, sent, groups):
    terms, done = [value], 1
    while done < groups:
        if done > 1:
            value = functools.reduce(jnp.add, terms)
            sent = value.astype(sent.dtype)
        masks = (1, 2, 3) if groups // done >= 4 else (1,)
        terms = [value]
        for mask in masks:
            pairs = [(g, g ^ (mask * done)) for g in range(groups)]
            terms.append(lax.ppermute(sent, "member", pairs))
        done *= len(masks) + 1
    return terms


def after(value, *others):
    return lax.optimization_barrier((value, *others))[0]


def resident(value):
    return pltpu.with_memory_space_constraint(value, pltpu.VMEM)


def call(body, meta, operands, outs, name, scratch=(), spaces=None):
    spaces = spaces or [pltpu.VMEM] * len(operands)
    return pl.pallas_call(
        body,
        in_specs=[pl.BlockSpec(memory_space=pltpu.SMEM)]
        + [pl.BlockSpec(memory_space=space) for space in spaces],
        out_specs=[pl.BlockSpec(memory_space=pltpu.VMEM) for _ in outs],
        out_shape=outs,
        scratch_shapes=scratch,
        compiler_params=pltpu.CompilerParams(vmem_limit_bytes=VMEM_LIMIT),
        cost_estimate=pl.CostEstimate(flops=0, bytes_accessed=0, transcendentals=0),
        name=name,
    )(meta, *operands)


def times(rows, block):
    return jnp.dot(rows, block, preferred_element_type=jnp.float32)


def times_transposed(rows, block):
    return lax.dot_general(
        rows, block, (((1,), (1,)), ((), ())), preferred_element_type=jnp.float32
    )


def add_times(meta, held, place, rows, out):
    @pl.when(meta[place] > 0)
    def _():
        out[...] += times(rows[...], held[place])


def load(chunks, meta, blocks, perturb, innovation, weight, *refs):
    own, outs = refs[:chunks], refs[chunks:2 * chunks]
    held, held_perturb, held_innovation, held_weight, turned, arrived = refs[2 * chunks:]
    slots = held.shape[0]
    copies = [
        pltpu.make_async_copy(blocks.at[0, meta[slots + k]], held.at[k], arrived.at[k])
        for k in range(slots)
    ]
    copies += [
        pltpu.make_async_copy(source, target, arrived.at[slots + k])
        for k, (source, target) in enumerate((
            (perturb, held_perturb), (innovation, held_innovation), (weight, held_weight),
        ))
    ]
    for copy in copies:
        copy.start()
    for out in outs:
        out[...] = jnp.zeros_like(out)
    copies[OWN].wait()
    for rows, out in zip(own, outs):
        add_times(meta, held, OWN, rows, out)
    for k, place in enumerate(TURNED):
        copies[place].wait()

        @pl.when(meta[place] > 0)
        def _(k=k, place=place):
            turned[k] = held[place].T

    for k, copy in enumerate(copies):
        if k not in (OWN, *TURNED):
            copy.wait()


def forward_add(chunk, places, meta, held, before, *refs):
    out = refs[-1]
    out[...] = before[...]
    count = out.shape[0]
    for place, rows in zip(places, refs):
        if rows.shape[0] > count:
            rows = rows.at[chunk * count:(chunk + 1) * count]
        add_times(meta, held, place, rows, out)


def forward_far(chunk, meta, held, perturb, before, swapped, out, sent, total):
    levels = out.shape[1]
    at = slice(chunk * levels, (chunk + 1) * levels)
    total[...] = before[...]
    add_times(meta, held, SWAPPED, swapped, total)
    for t in range(out.shape[0]):
        value = sum(
            perturb[t, m, at].astype(jnp.float32) * total[m * levels:(m + 1) * levels]
            for m in range(perturb.shape[1])
        )
        out[t] = value
        sent[t] = value.astype(sent.dtype)


def back_times(held, turned, place, rows):
    if place in TURNED:
        return times(rows[...], turned[TURNED.index(place)])
    return times_transposed(rows[...], held[place])


def transposed_or_zero(meta, held, turned, place, rows, *outs):
    size = outs[0].shape[0]
    alive = meta[place] > 0

    @pl.when(alive)
    def _():
        value = back_times(held, turned, place, rows)
        for k, out in enumerate(outs):
            out[...] = value[k * size:(k + 1) * size].astype(out.dtype)

    @pl.when(jnp.logical_not(alive))
    def _():
        for out in outs:
            out[...] = jnp.zeros_like(out)


def backward_first(chunk, pieces, meta, turned, perturb, innovation, weight, *refs):
    terms, refs = refs[:-4 - pieces], refs[-4 - pieces:]
    adjoint_in, *swap, direct, part, summed = refs
    slots = len(ORDER)
    count, levels, cells = summed.shape
    width = part.shape[-1]
    at = slice(chunk * levels, (chunk + 1) * levels)
    seen = lax.broadcasted_iota(jnp.int32, (levels, cells), 1) < meta[2 * slots]
    residual = []
    for t in range(count):
        value = sum(term[t].astype(jnp.float32) for term in terms)
        summed[t] = value
        residual.append(weight[at] * jnp.where(seen, value - innovation[t, at], 0.0))
    part[...] = summed[:, :, pl.ds(pl.multiple_of(meta[2 * slots + 1] * width, 128), width)]
    for m in range(perturb.shape[1]):
        value = sum(perturb[t, m, at].astype(jnp.float32) * residual[t] for t in range(count))
        adjoint_in[m * levels:(m + 1) * levels] = value.astype(adjoint_in.dtype)
    transposed_or_zero(meta, None, turned, SWAPPED, adjoint_in, *swap)
    transposed_or_zero(meta, None, turned, LATE, adjoint_in, direct)


def backward_through(meta, turned, adjoint_in, *refs):
    *swap, out = refs
    size = swap[0].shape[0]
    alive = meta[EARLY] > 0

    @pl.when(alive)
    def _():
        value = back_times(None, turned, EARLY, adjoint_in)
        for k, piece in enumerate(swap):
            at = slice(k * size, (k + 1) * size)
            out[at] = (value[at] + piece[...].astype(jnp.float32)).astype(out.dtype)

    @pl.when(jnp.logical_not(alive))
    def _():
        for k, piece in enumerate(swap):
            out[k * size:(k + 1) * size] = piece[...]


def backward_rest(meta, held, adjoint_in, *outs):
    transposed_or_zero(meta, held, None, PARTNER, adjoint_in, *outs[:-1])
    transposed_or_zero(meta, held, None, OWN, adjoint_in, outs[-1])


def finish(pieces, coeffs, kept, direct, through, *refs):
    second, out = refs[:pieces], refs[-1]
    value = kept[...] + jnp.concatenate([v[...].astype(jnp.float32) for v in second])
    for term in (direct, through):
        value = value + term[...].astype(jnp.float32)
    out[...] = coeffs[...] + value.reshape(out.shape)


def shards(coeffs, perturb, blocks, neighbours, live, obs_count, innovation, obs_weight):
    members, levels, cells = coeffs.shape
    window = perturb.shape[0]
    slots = blocks.shape[1]
    tile_count = lax.axis_size("tile")
    groups = lax.axis_size("member")
    tile_index = lax.axis_index("tile")
    group_index = lax.axis_index("member")
    half, full = jnp.bfloat16, jnp.float32
    part = levels // CHUNKS
    rows = members * part
    width = cells // groups
    shape = jax.ShapeDtypeStruct
    rows_half, rows_full = shape((rows, cells), half), shape((rows, cells), full)

    side = 1 - 2 * (tile_index % 2)
    radius = (slots - 1) // 2
    offset = (neighbours[0] - tile_index) % tile_count
    offset = jnp.where(offset > radius, offset - tile_count, offset) * side
    match = offset[None, :] == jnp.array(ORDER, jnp.int32)[:, None]
    slot = jnp.sum(jnp.where(match, jnp.arange(slots)[None, :], 0), axis=1)
    meta = jnp.concatenate(
        [(slot < live[0]).astype(slot.dtype), slot, obs_count, group_index[None]]
    ).astype(jnp.int32)

    inward = shift_pairs(tile_count, lambda core: -2 if core == 0 else 2)
    outward = shift_pairs(tile_count, lambda core: 2 if core == 0 else -2)
    across = shift_pairs(tile_count, lambda core: 1 if core == 0 else -1)

    own = []
    for c in range(CHUNKS):
        source = coeffs if c == 0 else after(coeffs, own[c - 1])
        own.append(source[:, c * part:(c + 1) * part].astype(half).reshape(rows, cells))
    distant = [
        pltpu.with_memory_space_constraint(v, pltpu.HBM)
        for v in (blocks, perturb, innovation, obs_weight)
    ]
    *near, held, held_perturb, held_innovation, held_weight, turned = call(
        functools.partial(load, CHUNKS), meta, (*distant, *own),
        [rows_full] * CHUNKS
        + [pltpu.VMEM(v.shape, v.dtype) for v in (blocks[0], perturb, innovation, obs_weight)]
        + [pltpu.VMEM((len(TURNED), cells, cells), half)],
        "load", [pltpu.SemaphoreType.DMA((slots + 3,))],
        [pltpu.HBM] * 4 + [pltpu.VMEM] * CHUNKS,
    )
    held, held_perturb, held_innovation, held_weight, turned = map(
        resident, (held, held_perturb, held_innovation, held_weight, turned)
    )

    def add(c, before, name, **rows):
        places = tuple(PLACES[key] for key in rows)
        [total] = call(
            functools.partial(forward_add, c, places), meta, (held, before, *rows.values()), [rows_full], name
        )
        return total

    def observe(c, total, swapped):
        return call(
            functools.partial(forward_far, c), meta, (held, held_perturb, total, swapped),
            [shape((window, part, cells), full), shape((window, part, cells), half)],
            "forward_far", [pltpu.VMEM((rows, cells), full)],
        )

    def cut(pieces):
        return [shape((rows // pieces, cells), half)] * pieces

    def respond(c, pieces, terms, *others):
        adjoint_in, *swap, direct, increment = call(
            functools.partial(backward_first, c, pieces), meta,
            (turned, held_perturb, held_innovation, held_weight, after(terms[0], *others), *terms[1:]),
            [rows_half, *cut(pieces), rows_half, shape((window, part, width), full)],
            "backward_first", [pltpu.VMEM((window, part, cells), full)],
        )
        return adjoint_in, swap, direct, increment

    def add_through(adjoint_in, swap):
        [through] = call(backward_through, meta, (turned, adjoint_in, *swap), [rows_half], "backward_through")
        return through

    def rest(pieces, adjoint_in, *others):
        *second, kept = call(
            backward_rest, meta, (held, after(adjoint_in, *others)), [*cut(pieces), rows_full],
            "backward_rest",
        )
        return second, kept

    def finished(c, gradient, second, *terms):
        terms += tuple(second)
        chunk_spec = pl.BlockSpec((members, part, cells), lambda i: (0, c, 0))
        return pl.pallas_call(
            functools.partial(finish, len(second)),
            grid=(1,),
            in_specs=[chunk_spec] + [pl.BlockSpec(v.shape, lambda i: (0, 0)) for v in terms]
            + [pl.BlockSpec(memory_space=pl.ANY)] * len(gradient),
            out_specs=chunk_spec,
            out_shape=shape(coeffs.shape, full),
            input_output_aliases={1 + len(terms): 0} if gradient else {},
            compiler_params=pltpu.CompilerParams(vmem_limit_bytes=VMEM_LIMIT),
            cost_estimate=pl.CostEstimate(flops=0, bytes_accessed=0, transcendentals=0),
            name="finish",
        )(coeffs, *terms, *gradient)

    early0 = lax.ppermute(own[0], "tile", inward)
    late0 = lax.ppermute(own[0], "tile", outward)
    partner = lax.ppermute(jnp.concatenate(after(own, near[0])), "tile", across)
    swapped0 = lax.ppermute(after(early0, late0, near[0]), "tile", across)
    early1 = lax.ppermute(after(own[1], early0, late0), "tile", inward)
    late1 = lax.ppermute(after(own[1], early0, late0), "tile", outward)
    total0 = add(0, near[0], "forward_mid", partner=partner, early=early0, late=late0)
    increment0, sent0 = observe(0, total0, swapped0)
    terms0 = member_terms(increment0, sent0, groups)
    near1 = add(1, near[1], "forward_near", partner=partner)
    adjoint0, swap0, direct0, part0 = respond(0, 1, terms0, near1)
    swap0 = [lax.ppermute(v, "tile", across) for v in swap0]
    direct0 = lax.ppermute(direct0, "tile", inward)
    swapped1 = lax.ppermute(after(early1, late1, adjoint0), "tile", across)
    total1 = add(1, near1, "forward_mid", early=early1, late=late1)
    increment1, sent1 = observe(1, total1, swapped1)
    through0 = add_through(adjoint0, swap0)
    second0, kept0 = rest(1, adjoint0, through0)
    through0 = lax.ppermute(through0, "tile", outward)
    second0 = [lax.ppermute(v, "tile", across) for v in second0]
    terms1 = member_terms(increment1, sent1, groups)
    adjoint1, swap1, direct1, part1 = respond(1, 2, terms1, kept0)
    swap1 = [lax.ppermute(v, "tile", across) for v in swap1]
    direct1 = lax.ppermute(direct1, "tile", inward)
    through1 = lax.ppermute(add_through(after(adjoint1, through0, direct0), swap1), "tile", outward)
    second1, kept1 = rest(2, adjoint1, *swap1)
    second1 = [lax.ppermute(v, "tile", across) for v in second1]
    gradient = finished(0, (), second0, kept0, direct0, through0)
    gradient = finished(1, (gradient,), second1, kept1, direct1, through1)
    return (jnp.concatenate((part0, part1), axis=1), gradient)


def solution(mesh):
    placed = (
        P("member", None, "tile"),
        P(None, "member", None, "tile"),
        P("tile", None, None, None),
        P("tile", None),
        P("tile"),
        P("tile"),
        P(None, None, "tile"),
        P(None, "tile"),
    )
    return jax.shard_map(
        shards,
        mesh=mesh,
        in_specs=placed,
        out_specs=(P(None, None, ("tile", "member")), P("member", None, "tile")),
        check_vma=False,
    )
```

```python
import functools
import jax
import jax.numpy as jnp
from jax import lax
from jax.experimental import pallas as pl
from jax.experimental.pallas import tpu as pltpu
from jax.sharding import PartitionSpec as P

CHUNKS = 2
HEAVY = 100 * 10**9
VMEM_LIMIT = 20 * 1024 * 1024
OWN, PARTNER, EARLY, SWAPPED, LATE = range(5)
PLACES = {"partner": PARTNER, "early": EARLY, "late": LATE}
ORDER = (0, 1, 2, -1, -2)
TURNED = (SWAPPED, LATE, EARLY)


def shift_pairs(count, step):
    return [(source, (source + step(source % 2)) % count) for source in range(count)]


def member_terms(value, sent, groups):
    terms, done = [value], 1
    while done < groups:
        if done > 1:
            value = functools.reduce(jnp.add, terms)
            sent = value.astype(sent.dtype)
        masks = (1, 2, 3) if groups // done >= 4 else (1,)
        terms = [value]
        for mask in masks:
            pairs = [(g, g ^ (mask * done)) for g in range(groups)]
            terms.append(lax.ppermute(sent, "member", pairs))
        done *= len(masks) + 1
    return terms


def after(value, *others):
    return lax.optimization_barrier((value, *others))[0]


def resident(value):
    return pltpu.with_memory_space_constraint(value, pltpu.VMEM)


def call(body, meta, operands, outs, name, scratch=(), spaces=None, flops=0):
    spaces = spaces or [pltpu.VMEM] * len(operands)
    return pl.pallas_call(
        body,
        in_specs=[pl.BlockSpec(memory_space=pltpu.SMEM)]
        + [pl.BlockSpec(memory_space=space) for space in spaces],
        out_specs=[pl.BlockSpec(memory_space=pltpu.VMEM) for _ in outs],
        out_shape=outs,
        scratch_shapes=scratch,
        compiler_params=pltpu.CompilerParams(vmem_limit_bytes=VMEM_LIMIT),
        cost_estimate=pl.CostEstimate(flops=flops, bytes_accessed=0, transcendentals=0),
        name=name,
    )(meta, *operands)


def times(rows, block):
    return jnp.dot(rows, block, preferred_element_type=jnp.float32)


def times_transposed(rows, block):
    return lax.dot_general(
        rows, block, (((1,), (1,)), ((), ())), preferred_element_type=jnp.float32
    )


def add_times(meta, held, place, rows, out):
    @pl.when(meta[place] > 0)
    def _():
        out[...] += times(rows[...], held[place])


def load(chunks, meta, blocks, perturb, innovation, weight, *refs):
    own, outs = refs[:chunks], refs[chunks:2 * chunks]
    held, held_perturb, held_innovation, held_weight, turned, arrived = refs[2 * chunks:]
    slots = held.shape[0]
    copies = [
        pltpu.make_async_copy(blocks.at[0, meta[slots + k]], held.at[k], arrived.at[k])
        for k in range(slots)
    ]
    copies += [
        pltpu.make_async_copy(source, target, arrived.at[slots + k])
        for k, (source, target) in enumerate((
            (perturb, held_perturb), (innovation, held_innovation), (weight, held_weight),
        ))
    ]
    for copy in copies:
        copy.start()
    for out in outs:
        out[...] = jnp.zeros_like(out)
    copies[OWN].wait()
    for rows, out in zip(own, outs):
        add_times(meta, held, OWN, rows, out)
    for k, place in enumerate(TURNED):
        copies[place].wait()

        @pl.when(meta[place] > 0)
        def _(k=k, place=place):
            turned[k] = held[place].T

    for k, copy in enumerate(copies):
        if k not in (OWN, *TURNED):
            copy.wait()


def forward_add(chunk, places, meta, held, before, *refs):
    out = refs[-1]
    out[...] = before[...]
    count = out.shape[0]
    for place, rows in zip(places, refs):
        if rows.shape[0] > count:
            rows = rows.at[chunk * count:(chunk + 1) * count]
        add_times(meta, held, place, rows, out)


def forward_far(chunk, meta, held, perturb, before, swapped, out, sent, total):
    levels = out.shape[1]
    at = slice(chunk * levels, (chunk + 1) * levels)
    total[...] = before[...]
    add_times(meta, held, SWAPPED, swapped, total)
    for t in range(out.shape[0]):
        value = sum(
            perturb[t, m, at].astype(jnp.float32) * total[m * levels:(m + 1) * levels]
            for m in range(perturb.shape[1])
        )
        out[t] = value
        sent[t] = value.astype(sent.dtype)


def back_times(held, turned, place, rows):
    if place in TURNED:
        return times(rows[...], turned[TURNED.index(place)])
    return times_transposed(rows[...], held[place])


def transposed_or_zero(meta, held, turned, place, rows, *outs):
    size = outs[0].shape[0]
    alive = meta[place] > 0

    @pl.when(alive)
    def _():
        value = back_times(held, turned, place, rows)
        for k, out in enumerate(outs):
            out[...] = value[k * size:(k + 1) * size].astype(out.dtype)

    @pl.when(jnp.logical_not(alive))
    def _():
        for out in outs:
            out[...] = jnp.zeros_like(out)


def backward_first(chunk, pieces, meta, turned, perturb, innovation, weight, *refs):
    terms, refs = refs[:-4 - pieces], refs[-4 - pieces:]
    adjoint_in, *swap, direct, part, summed = refs
    slots = len(ORDER)
    count, levels, cells = summed.shape
    width = part.shape[-1]
    at = slice(chunk * levels, (chunk + 1) * levels)
    seen = lax.broadcasted_iota(jnp.int32, (levels, cells), 1) < meta[2 * slots]
    residual = []
    for t in range(count):
        value = sum(term[t].astype(jnp.float32) for term in terms)
        summed[t] = value
        residual.append(weight[at] * jnp.where(seen, value - innovation[t, at], 0.0))
    part[...] = summed[:, :, pl.ds(pl.multiple_of(meta[2 * slots + 1] * width, 128), width)]
    for m in range(perturb.shape[1]):
        value = sum(perturb[t, m, at].astype(jnp.float32) * residual[t] for t in range(count))
        adjoint_in[m * levels:(m + 1) * levels] = value.astype(adjoint_in.dtype)
    transposed_or_zero(meta, None, turned, SWAPPED, adjoint_in, *swap)
    transposed_or_zero(meta, None, turned, LATE, adjoint_in, direct)


def backward_through(meta, turned, adjoint_in, *refs):
    *swap, out = refs
    size = swap[0].shape[0]
    alive = meta[EARLY] > 0

    @pl.when(alive)
    def _():
        value = back_times(None, turned, EARLY, adjoint_in)
        for k, piece in enumerate(swap):
            at = slice(k * size, (k + 1) * size)
            out[at] = (value[at] + piece[...].astype(jnp.float32)).astype(out.dtype)

    @pl.when(jnp.logical_not(alive))
    def _():
        for k, piece in enumerate(swap):
            out[k * size:(k + 1) * size] = piece[...]


def backward_rest(meta, held, adjoint_in, *outs):
    transposed_or_zero(meta, held, None, PARTNER, adjoint_in, *outs[:-1])
    transposed_or_zero(meta, held, None, OWN, adjoint_in, outs[-1])


def finish(pieces, coeffs, kept, direct, through, *refs):
    second, out = refs[:pieces], refs[-1]
    value = kept[...] + jnp.concatenate([v[...].astype(jnp.float32) for v in second])
    for term in (direct, through):
        value = value + term[...].astype(jnp.float32)
    out[...] = coeffs[...] + value.reshape(out.shape)


def shards(coeffs, perturb, blocks, neighbours, live, obs_count, innovation, obs_weight):
    members, levels, cells = coeffs.shape
    window = perturb.shape[0]
    slots = blocks.shape[1]
    tile_count = lax.axis_size("tile")
    groups = lax.axis_size("member")
    tile_index = lax.axis_index("tile")
    group_index = lax.axis_index("member")
    half, full = jnp.bfloat16, jnp.float32
    part = levels // CHUNKS
    rows = members * part
    width = cells // groups
    shape = jax.ShapeDtypeStruct
    rows_half, rows_full = shape((rows, cells), half), shape((rows, cells), full)

    side = 1 - 2 * (tile_index % 2)
    radius = (slots - 1) // 2
    offset = (neighbours[0] - tile_index) % tile_count
    offset = jnp.where(offset > radius, offset - tile_count, offset) * side
    match = offset[None, :] == jnp.array(ORDER, jnp.int32)[:, None]
    slot = jnp.sum(jnp.where(match, jnp.arange(slots)[None, :], 0), axis=1)
    meta = jnp.concatenate(
        [(slot < live[0]).astype(slot.dtype), slot, obs_count, group_index[None]]
    ).astype(jnp.int32)

    inward = shift_pairs(tile_count, lambda core: -2 if core == 0 else 2)
    outward = shift_pairs(tile_count, lambda core: 2 if core == 0 else -2)
    across = shift_pairs(tile_count, lambda core: 1 if core == 0 else -1)

    own = []
    for c in range(CHUNKS):
        source = coeffs if c == 0 else after(coeffs, own[c - 1])
        own.append(source[:, c * part:(c + 1) * part].astype(half).reshape(rows, cells))
    distant = [
        pltpu.with_memory_space_constraint(v, pltpu.HBM)
        for v in (blocks, perturb, innovation, obs_weight)
    ]
    *near, held, held_perturb, held_innovation, held_weight, turned = call(
        functools.partial(load, CHUNKS), meta, (*distant, *own),
        [rows_full] * CHUNKS
        + [pltpu.VMEM(v.shape, v.dtype) for v in (blocks[0], perturb, innovation, obs_weight)]
        + [pltpu.VMEM((len(TURNED), cells, cells), half)],
        "load", [pltpu.SemaphoreType.DMA((slots + 3,))],
        [pltpu.HBM] * 4 + [pltpu.VMEM] * CHUNKS,
    )
    held, held_perturb, held_innovation, held_weight, turned = map(
        resident, (held, held_perturb, held_innovation, held_weight, turned)
    )

    def add(c, before, name, **rows):
        places = tuple(PLACES[key] for key in rows)
        [total] = call(
            functools.partial(forward_add, c, places), meta, (held, before, *rows.values()), [rows_full], name
        )
        return total

    def observe(c, total, swapped):
        return call(
            functools.partial(forward_far, c), meta, (held, held_perturb, total, swapped),
            [shape((window, part, cells), full), shape((window, part, cells), half)],
            "forward_far", [pltpu.VMEM((rows, cells), full)],
        )

    def cut(pieces):
        return [shape((rows // pieces, cells), half)] * pieces

    def respond(c, pieces, terms, *others):
        adjoint_in, *swap, direct, increment = call(
            functools.partial(backward_first, c, pieces), meta,
            (turned, held_perturb, held_innovation, held_weight, after(terms[0], *others), *terms[1:]),
            [rows_half, *cut(pieces), rows_half, shape((window, part, width), full)],
            "backward_first", [pltpu.VMEM((window, part, cells), full)],
        )
        return adjoint_in, swap, direct, increment

    def add_through(adjoint_in, swap):
        [through] = call(backward_through, meta, (turned, adjoint_in, *swap), [rows_half], "backward_through")
        return through

    def rest(pieces, adjoint_in, *others, flops=0):
        *second, kept = call(
            backward_rest, meta, (held, after(adjoint_in, *others)), [*cut(pieces), rows_full],
            "backward_rest", flops=flops,
        )
        return second, kept

    def finished(c, gradient, second, *terms):
        terms += tuple(second)
        chunk_spec = pl.BlockSpec((members, part, cells), lambda i: (0, c, 0))
        return pl.pallas_call(
            functools.partial(finish, len(second)),
            grid=(1,),
            in_specs=[chunk_spec] + [pl.BlockSpec(v.shape, lambda i: (0, 0)) for v in terms]
            + [pl.BlockSpec(memory_space=pl.ANY)] * len(gradient),
            out_specs=chunk_spec,
            out_shape=shape(coeffs.shape, full),
            input_output_aliases={1 + len(terms): 0} if gradient else {},
            compiler_params=pltpu.CompilerParams(vmem_limit_bytes=VMEM_LIMIT),
            cost_estimate=pl.CostEstimate(flops=0, bytes_accessed=0, transcendentals=0),
            name="finish",
        )(coeffs, *terms, *gradient)

    early0 = lax.ppermute(own[0], "tile", inward)
    late0 = lax.ppermute(own[0], "tile", outward)
    partner = lax.ppermute(jnp.concatenate(after(own, near[0])), "tile", across)
    swapped0 = lax.ppermute(after(early0, late0, near[0]), "tile", across)
    early1 = lax.ppermute(after(own[1], early0, late0), "tile", inward)
    late1 = lax.ppermute(after(own[1], early0, late0), "tile", outward)
    total0 = add(0, near[0], "forward_mid", partner=partner, early=early0, late=late0)
    increment0, sent0 = observe(0, total0, swapped0)
    terms0 = member_terms(increment0, sent0, groups)
    near1 = add(1, near[1], "forward_near", partner=partner)
    adjoint0, swap0, direct0, part0 = respond(0, 1, terms0, near1)
    swap0 = [lax.ppermute(v, "tile", across) for v in swap0]
    direct0 = lax.ppermute(direct0, "tile", inward)
    swapped1 = lax.ppermute(after(early1, late1, adjoint0), "tile", across)
    total1 = add(1, near1, "forward_mid", early=early1, late=late1)
    increment1, sent1 = observe(1, total1, swapped1)
    through0 = add_through(adjoint0, swap0)
    second0, kept0 = rest(1, adjoint0, through0, direct0, flops=HEAVY)
    through0 = lax.ppermute(through0, "tile", outward)
    second0 = [lax.ppermute(v, "tile", across) for v in second0]
    terms1 = member_terms(increment1, sent1, groups)
    adjoint1, swap1, direct1, part1 = respond(1, 2, terms1, kept0)
    swap1 = [lax.ppermute(v, "tile", across) for v in swap1]
    direct1 = lax.ppermute(direct1, "tile", inward)
    through1 = lax.ppermute(add_through(after(adjoint1, through0, direct0), swap1), "tile", outward)
    second1, kept1 = rest(2, adjoint1, *swap1)
    second1 = [lax.ppermute(v, "tile", across) for v in second1]
    gradient = finished(0, (), second0, kept0, direct0, through0)
    gradient = finished(1, (gradient,), second1, kept1, direct1, through1)
    return (jnp.concatenate((part0, part1), axis=1), gradient)


def solution(mesh):
    placed = (
        P("member", None, "tile"),
        P(None, "member", None, "tile"),
        P("tile", None, None, None),
        P("tile", None),
        P("tile"),
        P("tile"),
        P(None, None, "tile"),
        P(None, "tile"),
    )
    return jax.shard_map(
        shards,
        mesh=mesh,
        in_specs=placed,
        out_specs=(P(None, None, ("tile", "member")), P("member", None, "tile")),
        check_vma=False,
    )
```

```python
import functools
import jax
import jax.numpy as jnp
from jax import lax
from jax.experimental import pallas as pl
from jax.experimental.pallas import tpu as pltpu
from jax.sharding import PartitionSpec as P

CHUNKS = 2
HEAVY = 100 * 10**9
VMEM_LIMIT = 20 * 1024 * 1024
OWN, PARTNER, EARLY, SWAPPED, LATE = range(5)
PLACES = {"partner": PARTNER, "early": EARLY, "late": LATE}
ORDER = (0, 1, 2, -1, -2)
TURNED = (SWAPPED, LATE, EARLY)


def shift_pairs(count, step):
    return [(source, (source + step(source % 2)) % count) for source in range(count)]


def member_terms(value, sent, groups):
    terms, done = [value], 1
    while done < groups:
        if done > 1:
            value = functools.reduce(jnp.add, terms)
            sent = value.astype(sent.dtype)
        masks = (1, 2, 3) if groups // done >= 4 else (1,)
        terms = [value]
        for mask in masks:
            pairs = [(g, g ^ (mask * done)) for g in range(groups)]
            terms.append(lax.ppermute(sent, "member", pairs))
        done *= len(masks) + 1
    return terms


def after(value, *others):
    return lax.optimization_barrier((value, *others))[0]


def resident(value):
    return pltpu.with_memory_space_constraint(value, pltpu.VMEM)


def call(body, meta, operands, outs, name, scratch=(), spaces=None, flops=0):
    spaces = spaces or [pltpu.VMEM] * len(operands)
    return pl.pallas_call(
        body,
        in_specs=[pl.BlockSpec(memory_space=pltpu.SMEM)]
        + [pl.BlockSpec(memory_space=space) for space in spaces],
        out_specs=[pl.BlockSpec(memory_space=pltpu.VMEM) for _ in outs],
        out_shape=outs,
        scratch_shapes=scratch,
        compiler_params=pltpu.CompilerParams(vmem_limit_bytes=VMEM_LIMIT),
        cost_estimate=pl.CostEstimate(flops=flops, bytes_accessed=0, transcendentals=0),
        name=name,
    )(meta, *operands)


def times(rows, block):
    return jnp.dot(rows, block, preferred_element_type=jnp.float32)


def times_transposed(rows, block):
    return lax.dot_general(
        rows, block, (((1,), (1,)), ((), ())), preferred_element_type=jnp.float32
    )


def add_times(meta, held, place, rows, out):
    @pl.when(meta[place] > 0)
    def _():
        out[...] += times(rows[...], held[place])


def load(chunks, meta, blocks, perturb, innovation, weight, *refs):
    own, outs = refs[:chunks], refs[chunks:2 * chunks]
    held, held_perturb, held_innovation, held_weight, turned, arrived = refs[2 * chunks:]
    slots = held.shape[0]
    copies = [
        pltpu.make_async_copy(blocks.at[0, meta[slots + k]], held.at[k], arrived.at[k])
        for k in range(slots)
    ]
    copies += [
        pltpu.make_async_copy(source, target, arrived.at[slots + k])
        for k, (source, target) in enumerate((
            (perturb, held_perturb), (innovation, held_innovation), (weight, held_weight),
        ))
    ]
    for copy in copies:
        copy.start()
    for out in outs:
        out[...] = jnp.zeros_like(out)
    copies[OWN].wait()
    for rows, out in zip(own, outs):
        add_times(meta, held, OWN, rows, out)
    for k, place in enumerate(TURNED):
        copies[place].wait()

        @pl.when(meta[place] > 0)
        def _(k=k, place=place):
            turned[k] = held[place].T

    for k, copy in enumerate(copies):
        if k not in (OWN, *TURNED):
            copy.wait()


def forward_add(chunk, places, meta, held, before, *refs):
    out = refs[-1]
    out[...] = before[...]
    count = out.shape[0]
    for place, rows in zip(places, refs):
        if rows.shape[0] > count:
            rows = rows.at[chunk * count:(chunk + 1) * count]
        add_times(meta, held, place, rows, out)


def forward_far(chunk, meta, held, perturb, before, *refs):
    *swapped, out, sent, total = refs
    levels = out.shape[1]
    at = slice(chunk * levels, (chunk + 1) * levels)
    total[...] = before[...]
    @pl.when(meta[SWAPPED] > 0)
    def _():
        rows = jnp.concatenate([v[...] for v in swapped])
        total[...] += times(rows, held[SWAPPED])

    for t in range(out.shape[0]):
        value = sum(
            perturb[t, m, at].astype(jnp.float32) * total[m * levels:(m + 1) * levels]
            for m in range(perturb.shape[1])
        )
        out[t] = value
        sent[t] = value.astype(sent.dtype)


def back_times(held, turned, place, rows):
    if place in TURNED:
        return times(rows[...], turned[TURNED.index(place)])
    return times_transposed(rows[...], held[place])


def transposed_or_zero(meta, held, turned, place, rows, *outs):
    size = outs[0].shape[0]
    alive = meta[place] > 0

    @pl.when(alive)
    def _():
        value = back_times(held, turned, place, rows)
        for k, out in enumerate(outs):
            out[...] = value[k * size:(k + 1) * size].astype(out.dtype)

    @pl.when(jnp.logical_not(alive))
    def _():
        for out in outs:
            out[...] = jnp.zeros_like(out)


def backward_first(chunk, pieces, meta, turned, perturb, innovation, weight, *refs):
    terms, refs = refs[:-4 - pieces], refs[-4 - pieces:]
    adjoint_in, *swap, direct, part, summed = refs
    slots = len(ORDER)
    count, levels, cells = summed.shape
    width = part.shape[-1]
    at = slice(chunk * levels, (chunk + 1) * levels)
    seen = lax.broadcasted_iota(jnp.int32, (levels, cells), 1) < meta[2 * slots]
    residual = []
    for t in range(count):
        value = sum(term[t].astype(jnp.float32) for term in terms)
        summed[t] = value
        residual.append(weight[at] * jnp.where(seen, value - innovation[t, at], 0.0))
    part[...] = summed[:, :, pl.ds(pl.multiple_of(meta[2 * slots + 1] * width, 128), width)]
    for m in range(perturb.shape[1]):
        value = sum(perturb[t, m, at].astype(jnp.float32) * residual[t] for t in range(count))
        adjoint_in[m * levels:(m + 1) * levels] = value.astype(adjoint_in.dtype)
    transposed_or_zero(meta, None, turned, SWAPPED, adjoint_in, *swap)
    transposed_or_zero(meta, None, turned, LATE, adjoint_in, direct)


def backward_through(meta, turned, adjoint_in, *refs):
    *swap, out = refs
    size = swap[0].shape[0]
    alive = meta[EARLY] > 0

    @pl.when(alive)
    def _():
        value = back_times(None, turned, EARLY, adjoint_in)
        for k, piece in enumerate(swap):
            at = slice(k * size, (k + 1) * size)
            out[at] = (value[at] + piece[...].astype(jnp.float32)).astype(out.dtype)

    @pl.when(jnp.logical_not(alive))
    def _():
        for k, piece in enumerate(swap):
            out[k * size:(k + 1) * size] = piece[...]


def backward_rest(meta, held, adjoint_in, *outs):
    transposed_or_zero(meta, held, None, PARTNER, adjoint_in, *outs[:-1])
    transposed_or_zero(meta, held, None, OWN, adjoint_in, outs[-1])


def backward_one(place, meta, held, adjoint_in, out):
    transposed_or_zero(meta, held, None, place, adjoint_in, out)


def settle(coeffs, *refs):
    *terms, out = refs
    value = coeffs[...].reshape(out.shape)
    if terms[0].shape == out.shape:
        value = value + terms[0][...].astype(jnp.float32)
        terms = terms[1:]
    if terms:
        value = value + jnp.concatenate([v[...].astype(jnp.float32) for v in terms])
    out[...] = value


def finish(chunk, terms, *refs):
    refs, (out, value, sent) = refs[:terms], refs[-3:]
    members, levels, _ = value.shape
    size = members // 2
    copies = []
    for k in range(2):
        rows = slice(k * size * levels, (k + 1) * size * levels)
        some = slice(k * size, (k + 1) * size)
        value[some] = sum(v[rows].astype(jnp.float32) for v in refs).reshape(size, levels, -1)
        copies.append(pltpu.make_async_copy(
            value.at[some], out.at[some, chunk * levels:(chunk + 1) * levels], sent.at[k]
        ))
        copies[k].start()
    for copy in copies:
        copy.wait()


def shards(coeffs, perturb, blocks, neighbours, live, obs_count, innovation, obs_weight):
    members, levels, cells = coeffs.shape
    window = perturb.shape[0]
    slots = blocks.shape[1]
    tile_count = lax.axis_size("tile")
    groups = lax.axis_size("member")
    tile_index = lax.axis_index("tile")
    group_index = lax.axis_index("member")
    half, full = jnp.bfloat16, jnp.float32
    part = levels // CHUNKS
    rows = members * part
    width = cells // groups
    shape = jax.ShapeDtypeStruct
    rows_half, rows_full = shape((rows, cells), half), shape((rows, cells), full)

    side = 1 - 2 * (tile_index % 2)
    radius = (slots - 1) // 2
    offset = (neighbours[0] - tile_index) % tile_count
    offset = jnp.where(offset > radius, offset - tile_count, offset) * side
    match = offset[None, :] == jnp.array(ORDER, jnp.int32)[:, None]
    slot = jnp.sum(jnp.where(match, jnp.arange(slots)[None, :], 0), axis=1)
    meta = jnp.concatenate(
        [(slot < live[0]).astype(slot.dtype), slot, obs_count, group_index[None]]
    ).astype(jnp.int32)

    inward = shift_pairs(tile_count, lambda core: -2 if core == 0 else 2)
    outward = shift_pairs(tile_count, lambda core: 2 if core == 0 else -2)
    across = shift_pairs(tile_count, lambda core: 1 if core == 0 else -1)

    own = []
    for c in range(CHUNKS):
        source = coeffs if c == 0 else after(coeffs, own[c - 1])
        own.append(source[:, c * part:(c + 1) * part].astype(half).reshape(rows, cells))
    distant = [
        pltpu.with_memory_space_constraint(v, pltpu.HBM)
        for v in (blocks, perturb, innovation, obs_weight)
    ]
    *near, held, held_perturb, held_innovation, held_weight, turned = call(
        functools.partial(load, CHUNKS), meta, (*distant, *own),
        [rows_full] * CHUNKS
        + [pltpu.VMEM(v.shape, v.dtype) for v in (blocks[0], perturb, innovation, obs_weight)]
        + [pltpu.VMEM((len(TURNED), cells, cells), half)],
        "load", [pltpu.SemaphoreType.DMA((slots + 3,))],
        [pltpu.HBM] * 4 + [pltpu.VMEM] * CHUNKS,
    )
    held, held_perturb, held_innovation, held_weight, turned = map(
        resident, (held, held_perturb, held_innovation, held_weight, turned)
    )

    def add(c, before, name, **rows):
        places = tuple(PLACES[key] for key in rows)
        [total] = call(
            functools.partial(forward_add, c, places), meta, (held, before, *rows.values()), [rows_full], name
        )
        return total

    def forwarded(pieces, early, *others):
        early, size = after(early, *others), rows // pieces
        return [lax.ppermute(early[k * size:(k + 1) * size], "tile", across) for k in range(pieces)]

    def observe(c, total, swapped):
        return call(
            functools.partial(forward_far, c), meta, (held, held_perturb, total, *swapped),
            [shape((window, part, cells), full), shape((window, part, cells), half)],
            "forward_far", [pltpu.VMEM((rows, cells), full)],
        )

    def cut(pieces):
        return [shape((rows // pieces, cells), half)] * pieces

    def respond(c, pieces, terms, *others):
        adjoint_in, *swap, direct, increment = call(
            functools.partial(backward_first, c, pieces), meta,
            (turned, held_perturb, held_innovation, held_weight, after(terms[0], *others), *terms[1:]),
            [rows_half, *cut(pieces), rows_half, shape((window, part, width), full)],
            "backward_first", [pltpu.VMEM((window, part, cells), full)],
        )
        return adjoint_in, swap, direct, increment

    def add_through(adjoint_in, swap):
        [through] = call(backward_through, meta, (turned, adjoint_in, *swap), [rows_half], "backward_through")
        return through

    def rest(pieces, adjoint_in, *others):
        *second, kept = call(
            backward_rest, meta, (held, after(adjoint_in, *others)), [*cut(pieces), rows_full],
            "backward_rest",
        )
        return second, kept

    def one(place, out, name, adjoint_in, *others, flops=0):
        [value] = call(
            functools.partial(backward_one, place), meta, (held, after(adjoint_in, *others)), [out], name,
            flops=flops,
        )
        return value

    def settled(c, *terms):
        return pl.pallas_call(
            settle,
            grid=(1,),
            in_specs=[pl.BlockSpec((members, part, cells), lambda i: (0, c, 0))]
            + [pl.BlockSpec(v.shape, lambda i: (0, 0)) for v in terms],
            out_specs=pl.BlockSpec((rows, cells), lambda i: (0, 0)),
            out_shape=rows_full,
            compiler_params=pltpu.CompilerParams(vmem_limit_bytes=VMEM_LIMIT),
            cost_estimate=pl.CostEstimate(flops=0, bytes_accessed=0, transcendentals=0),
            name="settle",
        )(coeffs, *terms)

    def finished(c, gradient, *terms):
        return pl.pallas_call(
            functools.partial(finish, c, len(terms)),
            in_specs=[pl.BlockSpec(memory_space=pltpu.VMEM)] * len(terms)
            + [pl.BlockSpec(memory_space=pl.ANY)] * len(gradient),
            out_specs=pl.BlockSpec(memory_space=pl.ANY),
            out_shape=shape(coeffs.shape, full),
            scratch_shapes=[pltpu.VMEM((members, part, cells), full), pltpu.SemaphoreType.DMA((2,))],
            input_output_aliases={len(terms): 0} if gradient else {},
            compiler_params=pltpu.CompilerParams(vmem_limit_bytes=VMEM_LIMIT),
            cost_estimate=pl.CostEstimate(flops=0, bytes_accessed=0, transcendentals=0),
            name="finish",
        )(*terms, *gradient)

    early0 = lax.ppermute(own[0], "tile", inward)
    late0 = lax.ppermute(own[0], "tile", outward)
    partner = lax.ppermute(jnp.concatenate(after(own, near[0])), "tile", across)
    swapped0 = forwarded(2, early0, late0, near[0])
    early1 = lax.ppermute(after(own[1], early0, late0), "tile", inward)
    late1 = lax.ppermute(after(own[1], early0, late0), "tile", outward)
    total0 = add(0, near[0], "forward_mid", partner=partner, early=early0, late=late0)
    increment0, sent0 = observe(0, total0, swapped0)
    terms0 = member_terms(increment0, sent0, groups)
    near1 = add(1, near[1], "forward_near", partner=partner)
    adjoint0, swap0, direct0, part0 = respond(0, 2, terms0, near1)
    swap0 = [lax.ppermute(v, "tile", across) for v in swap0]
    direct0 = lax.ppermute(direct0, "tile", inward)
    swapped1 = forwarded(2, early1, late1, adjoint0)
    total1 = add(1, near1, "forward_mid", early=early1, late=late1)
    increment1, sent1 = observe(1, total1, swapped1)
    through0 = add_through(adjoint0, swap0)
    second0 = one(PARTNER, rows_half, "backward_second", adjoint0, direct0, flops=HEAVY)
    through0 = lax.ppermute(through0, "tile", outward)
    terms1 = member_terms(increment1, sent1, groups)
    adjoint1, swap1, direct1, part1 = respond(1, 2, terms1, second0)
    swap1 = [lax.ppermute(v, "tile", across) for v in swap1]
    second0 = lax.ppermute(second0, "tile", across)
    direct1 = lax.ppermute(direct1, "tile", inward)
    through1 = lax.ppermute(add_through(adjoint1, swap1), "tile", outward)
    second1, kept1 = rest(2, adjoint1, *swap1, through0)
    second1 = [lax.ppermute(v, "tile", across) for v in second1]
    kept0 = one(OWN, rows_full, "backward_kept", adjoint0, *second1)
    found0 = settled(0, direct0)
    found1 = settled(1, kept1, *second1)
    gradient = finished(0, (), found0, kept0, second0, through0)
    gradient = finished(1, (gradient,), found1, direct1, through1)
    return (jnp.concatenate((part0, part1), axis=1), gradient)


def solution(mesh):
    placed = (
        P("member", None, "tile"),
        P(None, "member", None, "tile"),
        P("tile", None, None, None),
        P("tile", None),
        P("tile"),
        P("tile"),
        P(None, None, "tile"),
        P(None, "tile"),
    )
    return jax.shard_map(
        shards,
        mesh=mesh,
        in_specs=placed,
        out_specs=(P(None, None, ("tile", "member")), P("member", None, "tile")),
        check_vma=False,
    )
```

```python
import functools
import jax
import jax.numpy as jnp
from jax import lax
from jax.experimental import pallas as pl
from jax.experimental.pallas import tpu as pltpu
from jax.sharding import PartitionSpec as P

CHUNKS = 2
HEAVY = 100 * 10**9
VMEM_LIMIT = 20 * 1024 * 1024
OWN, PARTNER, EARLY, SWAPPED, LATE = range(5)
PLACES = {"partner": PARTNER, "below": (12,), "above": (13,)}
ORDER = (0, 1, 2, -1, -2)
TURNED = (SWAPPED, LATE, EARLY)


def shift_pairs(count, step):
    return [(tile, (tile + step(tile % 2, tile // 2)) % count) for tile in range(count)]


def member_terms(value, sent, groups):
    terms, done = [value], 1
    while done < groups:
        if done > 1:
            value = functools.reduce(jnp.add, terms)
            sent = value.astype(sent.dtype)
        masks = (1, 2, 3) if groups // done >= 4 else (1,)
        terms = [value]
        for mask in masks:
            pairs = [(g, g ^ (mask * done)) for g in range(groups)]
            terms.append(lax.ppermute(sent, "member", pairs))
        done *= len(masks) + 1
    return terms


def after(value, *others):
    return lax.optimization_barrier((value, *others))[0]


def resident(value):
    return pltpu.with_memory_space_constraint(value, pltpu.VMEM)


def call(body, meta, operands, outs, name, scratch=(), spaces=None, flops=0):
    spaces = spaces or [pltpu.VMEM] * len(operands)
    return pl.pallas_call(
        body,
        in_specs=[pl.BlockSpec(memory_space=pltpu.SMEM)]
        + [pl.BlockSpec(memory_space=space) for space in spaces],
        out_specs=[pl.BlockSpec(memory_space=pltpu.VMEM) for _ in outs],
        out_shape=outs,
        scratch_shapes=scratch,
        compiler_params=pltpu.CompilerParams(vmem_limit_bytes=VMEM_LIMIT),
        cost_estimate=pl.CostEstimate(flops=flops, bytes_accessed=0, transcendentals=0),
        name=name,
    )(meta, *operands)


def times(rows, block):
    return jnp.dot(rows, block, preferred_element_type=jnp.float32)


def times_transposed(rows, block):
    return lax.dot_general(
        rows, block, (((1,), (1,)), ((), ())), preferred_element_type=jnp.float32
    )


def add_times(meta, held, place, rows, out):
    @pl.when(meta[place] > 0)
    def _():
        out[...] += times(rows[...], held[place])


def load(chunks, meta, blocks, perturb, innovation, weight, *refs):
    own, outs = refs[:chunks], refs[chunks:2 * chunks]
    held, held_perturb, held_innovation, held_weight, turned, arrived = refs[2 * chunks:]
    slots = held.shape[0]
    copies = [
        pltpu.make_async_copy(blocks.at[0, meta[slots + k]], held.at[k], arrived.at[k])
        for k in range(slots)
    ]
    copies += [
        pltpu.make_async_copy(source, target, arrived.at[slots + k])
        for k, (source, target) in enumerate((
            (perturb, held_perturb), (innovation, held_innovation), (weight, held_weight),
        ))
    ]
    for copy in copies:
        copy.start()
    for out in outs:
        out[...] = jnp.zeros_like(out)
    copies[OWN].wait()
    for rows, out in zip(own, outs):
        add_times(meta, held, OWN, rows, out)
    for k, place in enumerate(TURNED):
        copies[place].wait()

        @pl.when(meta[place] > 0)
        def _(k=k, place=place):
            turned[k] = held[place].T

    for k, copy in enumerate(copies):
        if k not in (OWN, *TURNED):
            copy.wait()


def forward_add(chunk, places, meta, held, before, *refs):
    out = refs[-1]
    out[...] = before[...]
    count = out.shape[0]
    for place, rows in zip(places, refs):
        place = meta[place[0]] if isinstance(place, tuple) else place
        if rows.shape[0] > count:
            rows = rows.at[chunk * count:(chunk + 1) * count]
        add_times(meta, held, place, rows, out)


def forward_far(chunk, meta, held, perturb, before, *refs):
    *swapped, out, sent, total = refs
    levels = out.shape[1]
    at = slice(chunk * levels, (chunk + 1) * levels)
    total[...] = before[...]
    @pl.when(meta[SWAPPED] > 0)
    def _():
        rows = jnp.concatenate([v[...] for v in swapped])
        total[...] += times(rows, held[SWAPPED])

    for t in range(out.shape[0]):
        value = sum(
            perturb[t, m, at].astype(jnp.float32) * total[m * levels:(m + 1) * levels]
            for m in range(perturb.shape[1])
        )
        out[t] = value
        sent[t] = value.astype(sent.dtype)


def back_times(held, turned, place, rows):
    if place in TURNED:
        return times(rows[...], turned[TURNED.index(place)])
    return times_transposed(rows[...], held[place])


def transposed_or_zero(meta, held, turned, place, rows, *outs):
    size = outs[0].shape[0]
    alive = meta[place] > 0

    @pl.when(alive)
    def _():
        value = back_times(held, turned, place, rows)
        for k, out in enumerate(outs):
            out[...] = value[k * size:(k + 1) * size].astype(out.dtype)

    @pl.when(jnp.logical_not(alive))
    def _():
        for out in outs:
            out[...] = jnp.zeros_like(out)


def backward_first(chunk, pieces, meta, turned, perturb, innovation, weight, *refs):
    terms, refs = refs[:-4 - pieces], refs[-4 - pieces:]
    adjoint_in, *swap, direct, part, summed = refs
    slots = len(ORDER)
    count, levels, cells = summed.shape
    width = part.shape[-1]
    at = slice(chunk * levels, (chunk + 1) * levels)
    seen = lax.broadcasted_iota(jnp.int32, (levels, cells), 1) < meta[2 * slots]
    residual = []
    for t in range(count):
        value = sum(term[t].astype(jnp.float32) for term in terms)
        summed[t] = value
        residual.append(weight[at] * jnp.where(seen, value - innovation[t, at], 0.0))
    part[...] = summed[:, :, pl.ds(pl.multiple_of(meta[2 * slots + 1] * width, 128), width)]
    for m in range(perturb.shape[1]):
        value = sum(perturb[t, m, at].astype(jnp.float32) * residual[t] for t in range(count))
        adjoint_in[m * levels:(m + 1) * levels] = value.astype(adjoint_in.dtype)
    transposed_or_zero(meta, None, turned, SWAPPED, adjoint_in, *swap)
    transposed_or_zero(meta, None, turned, LATE, adjoint_in, direct)


def backward_through(meta, turned, adjoint_in, *refs):
    *swap, out = refs
    size = swap[0].shape[0]
    alive = meta[EARLY] > 0

    @pl.when(alive)
    def _():
        value = back_times(None, turned, EARLY, adjoint_in)
        for k, piece in enumerate(swap):
            at = slice(k * size, (k + 1) * size)
            out[at] = (value[at] + piece[...].astype(jnp.float32)).astype(out.dtype)

    @pl.when(jnp.logical_not(alive))
    def _():
        for k, piece in enumerate(swap):
            out[k * size:(k + 1) * size] = piece[...]


def backward_rest(meta, held, adjoint_in, *outs):
    transposed_or_zero(meta, held, None, PARTNER, adjoint_in, *outs[:-1])
    transposed_or_zero(meta, held, None, OWN, adjoint_in, outs[-1])


def backward_one(place, meta, held, adjoint_in, out):
    transposed_or_zero(meta, held, None, place, adjoint_in, out)


def settle(coeffs, *refs):
    *terms, out = refs
    value = coeffs[...].reshape(out.shape)
    if terms[0].shape == out.shape:
        value = value + terms[0][...].astype(jnp.float32)
        terms = terms[1:]
    if terms:
        value = value + jnp.concatenate([v[...].astype(jnp.float32) for v in terms])
    out[...] = value


def finish(chunk, terms, *refs):
    refs, (out, value, sent) = refs[:terms], refs[-3:]
    members, levels, _ = value.shape
    size = members // 2
    copies = []
    for k in range(2):
        rows = slice(k * size * levels, (k + 1) * size * levels)
        some = slice(k * size, (k + 1) * size)
        value[some] = sum(v[rows].astype(jnp.float32) for v in refs).reshape(size, levels, -1)
        copies.append(pltpu.make_async_copy(
            value.at[some], out.at[some, chunk * levels:(chunk + 1) * levels], sent.at[k]
        ))
        copies[k].start()
    for copy in copies:
        copy.wait()


def shards(coeffs, perturb, blocks, neighbours, live, obs_count, innovation, obs_weight):
    members, levels, cells = coeffs.shape
    window = perturb.shape[0]
    slots = blocks.shape[1]
    tile_count = lax.axis_size("tile")
    groups = lax.axis_size("member")
    tile_index = lax.axis_index("tile")
    group_index = lax.axis_index("member")
    half, full = jnp.bfloat16, jnp.float32
    part = levels // CHUNKS
    rows = members * part
    width = cells // groups
    shape = jax.ShapeDtypeStruct
    rows_half, rows_full = shape((rows, cells), half), shape((rows, cells), full)

    side = 1 - 2 * (tile_index % 2)
    radius = (slots - 1) // 2
    offset = (neighbours[0] - tile_index) % tile_count
    offset = jnp.where(offset > radius, offset - tile_count, offset) * side
    match = offset[None, :] == jnp.array(ORDER, jnp.int32)[:, None]
    slot = jnp.sum(jnp.where(match, jnp.arange(slots)[None, :], 0), axis=1)
    places = jnp.where((tile_index // 2) % 2 == 0, jnp.array([LATE, EARLY]), jnp.array([EARLY, LATE]))
    meta = jnp.concatenate(
        [(slot < live[0]).astype(slot.dtype), slot, obs_count, group_index[None], places]
    ).astype(jnp.int32)

    inward = shift_pairs(tile_count, lambda core, chip: -2 if core == 0 else 2)
    outward = shift_pairs(tile_count, lambda core, chip: 2 if core == 0 else -2)
    below = shift_pairs(tile_count, lambda core, chip: -2 if (core + chip) % 2 == 0 else 2)
    above = shift_pairs(tile_count, lambda core, chip: 2 if (core + chip) % 2 == 0 else -2)
    even = (tile_index // 2) % 2 == 0
    across = shift_pairs(tile_count, lambda core, chip: 1 if core == 0 else -1)

    own = []
    for c in range(CHUNKS):
        source = coeffs if c == 0 else after(coeffs, own[c - 1])
        own.append(source[:, c * part:(c + 1) * part].astype(half).reshape(rows, cells))
    distant = [
        pltpu.with_memory_space_constraint(v, pltpu.HBM)
        for v in (blocks, perturb, innovation, obs_weight)
    ]
    *near, held, held_perturb, held_innovation, held_weight, turned = call(
        functools.partial(load, CHUNKS), meta, (*distant, *own),
        [rows_full] * CHUNKS
        + [pltpu.VMEM(v.shape, v.dtype) for v in (blocks[0], perturb, innovation, obs_weight)]
        + [pltpu.VMEM((len(TURNED), cells, cells), half)],
        "load", [pltpu.SemaphoreType.DMA((slots + 3,))],
        [pltpu.HBM] * 4 + [pltpu.VMEM] * CHUNKS,
    )
    held, held_perturb, held_innovation, held_weight, turned = map(
        resident, (held, held_perturb, held_innovation, held_weight, turned)
    )

    def add(c, before, name, **rows):
        places = tuple(PLACES[key] for key in rows)
        [total] = call(
            functools.partial(forward_add, c, places), meta, (held, before, *rows.values()), [rows_full], name
        )
        return total

    def forwarded(pieces, below, above, other):
        below, above, _ = lax.optimization_barrier((below, above, other))
        size = rows // pieces
        cuts = [slice(k * size, (k + 1) * size) for k in range(pieces)]
        return [lax.ppermute(jnp.where(even, above[at], below[at]), "tile", across) for at in cuts]

    def observe(c, total, swapped):
        return call(
            functools.partial(forward_far, c), meta, (held, held_perturb, total, *swapped),
            [shape((window, part, cells), full), shape((window, part, cells), half)],
            "forward_far", [pltpu.VMEM((rows, cells), full)],
        )

    def cut(pieces):
        return [shape((rows // pieces, cells), half)] * pieces

    def respond(c, pieces, terms, *others):
        adjoint_in, *swap, direct, increment = call(
            functools.partial(backward_first, c, pieces), meta,
            (turned, held_perturb, held_innovation, held_weight, after(terms[0], *others), *terms[1:]),
            [rows_half, *cut(pieces), rows_half, shape((window, part, width), full)],
            "backward_first", [pltpu.VMEM((window, part, cells), full)],
        )
        return adjoint_in, swap, direct, increment

    def add_through(adjoint_in, swap, flops=0):
        [through] = call(
            backward_through, meta, (turned, adjoint_in, *swap), [rows_half], "backward_through", flops=flops
        )
        return through

    def rest(pieces, adjoint_in, *others):
        *second, kept = call(
            backward_rest, meta, (held, after(adjoint_in, *others)), [*cut(pieces), rows_full],
            "backward_rest",
        )
        return second, kept

    def one(place, out, name, adjoint_in, *others):
        [value] = call(
            functools.partial(backward_one, place), meta, (held, after(adjoint_in, *others)), [out], name
        )
        return value

    def settled(c, *terms):
        return pl.pallas_call(
            settle,
            grid=(1,),
            in_specs=[pl.BlockSpec((members, part, cells), lambda i: (0, c, 0))]
            + [pl.BlockSpec(v.shape, lambda i: (0, 0)) for v in terms],
            out_specs=pl.BlockSpec((rows, cells), lambda i: (0, 0)),
            out_shape=rows_full,
            compiler_params=pltpu.CompilerParams(vmem_limit_bytes=VMEM_LIMIT),
            cost_estimate=pl.CostEstimate(flops=0, bytes_accessed=0, transcendentals=0),
            name="settle",
        )(coeffs, *terms)

    def finished(c, gradient, *terms):
        return pl.pallas_call(
            functools.partial(finish, c, len(terms)),
            in_specs=[pl.BlockSpec(memory_space=pltpu.VMEM)] * len(terms)
            + [pl.BlockSpec(memory_space=pl.ANY)] * len(gradient),
            out_specs=pl.BlockSpec(memory_space=pl.ANY),
            out_shape=shape(coeffs.shape, full),
            scratch_shapes=[pltpu.VMEM((members, part, cells), full), pltpu.SemaphoreType.DMA((2,))],
            input_output_aliases={len(terms): 0} if gradient else {},
            compiler_params=pltpu.CompilerParams(vmem_limit_bytes=VMEM_LIMIT),
            cost_estimate=pl.CostEstimate(flops=0, bytes_accessed=0, transcendentals=0),
            name="finish",
        )(*terms, *gradient)

    below0 = lax.ppermute(own[0], "tile", below)
    above0 = lax.ppermute(own[0], "tile", above)
    partner = lax.ppermute(jnp.concatenate(after(own, near[0])), "tile", across)
    swapped0 = forwarded(2, below0, above0, near[0])
    below1 = lax.ppermute(after(own[1], below0, above0), "tile", below)
    above1 = lax.ppermute(after(own[1], below0, above0), "tile", above)
    total0 = add(0, near[0], "forward_mid", partner=partner, below=below0, above=above0)
    increment0, sent0 = observe(0, total0, swapped0)
    terms0 = member_terms(increment0, sent0, groups)
    near1 = add(1, near[1], "forward_near", partner=partner)
    adjoint0, swap0, direct0, part0 = respond(0, 1, terms0, near1)
    swap0 = [lax.ppermute(v, "tile", across) for v in swap0]
    direct0 = lax.ppermute(direct0, "tile", inward)
    swapped1 = forwarded(2, below1, above1, adjoint0)
    total1 = add(1, near1, "forward_mid", below=below1, above=above1)
    increment1, sent1 = observe(1, total1, swapped1)
    through0 = add_through(after(adjoint0, direct0), swap0, flops=HEAVY)
    terms1 = member_terms(increment1, sent1, groups)
    adjoint1, swap1, direct1, part1 = respond(1, 2, terms1, through0)
    through0 = lax.ppermute(through0, "tile", outward)
    swap1 = [lax.ppermute(v, "tile", across) for v in swap1]
    second0 = one(PARTNER, rows_half, "backward_second", adjoint0, *swap1)
    second0 = lax.ppermute(second0, "tile", across)
    direct1 = lax.ppermute(direct1, "tile", inward)
    through1 = lax.ppermute(add_through(adjoint1, swap1), "tile", outward)
    second1, kept1 = rest(2, adjoint1, *swap1, through0)
    second1 = [lax.ppermute(v, "tile", across) for v in second1]
    kept0 = one(OWN, rows_full, "backward_kept", adjoint0, *second1)
    found0 = settled(0, direct0)
    found1 = settled(1, kept1, *second1)
    gradient = finished(0, (), found0, kept0, second0, through0)
    gradient = finished(1, (gradient,), found1, direct1, through1)
    return (jnp.concatenate((part0, part1), axis=1), gradient)


def solution(mesh):
    placed = (
        P("member", None, "tile"),
        P(None, "member", None, "tile"),
        P("tile", None, None, None),
        P("tile", None),
        P("tile"),
        P("tile"),
        P(None, None, "tile"),
        P(None, "tile"),
    )
    return jax.shard_map(
        shards,
        mesh=mesh,
        in_specs=placed,
        out_specs=(P(None, None, ("tile", "member")), P("member", None, "tile")),
        check_vma=False,
    )
```

```python
import functools
import jax
import jax.numpy as jnp
from jax import lax
from jax.experimental import pallas as pl
from jax.experimental.pallas import tpu as pltpu
from jax.sharding import PartitionSpec as P

CHUNKS = 2
HEAVY = 100 * 10**9
VMEM_LIMIT = 20 * 1024 * 1024
OWN, PARTNER, EARLY, SWAPPED, LATE = range(5)
PLACES = {"partner": PARTNER, "below": (12,), "above": (13,)}
ORDER = (0, 1, 2, -1, -2)
TURNED = (SWAPPED, LATE, EARLY)


def shift_pairs(count, step):
    return [(tile, (tile + step(tile % 2, tile // 2)) % count) for tile in range(count)]


def member_terms(value, sent, groups):
    terms, done = [value], 1
    while done < groups:
        if done > 1:
            value = functools.reduce(jnp.add, terms)
            sent = value.astype(sent.dtype)
        masks = (1, 2, 3) if groups // done >= 4 else (1,)
        terms = [value]
        for mask in masks:
            pairs = [(g, g ^ (mask * done)) for g in range(groups)]
            terms.append(lax.ppermute(sent, "member", pairs))
        done *= len(masks) + 1
    return terms


def after(value, *others):
    return lax.optimization_barrier((value, *others))[0]


def resident(value):
    return pltpu.with_memory_space_constraint(value, pltpu.VMEM)


def call(body, meta, operands, outs, name, scratch=(), spaces=None, flops=0):
    spaces = spaces or [pltpu.VMEM] * len(operands)
    return pl.pallas_call(
        body,
        in_specs=[pl.BlockSpec(memory_space=pltpu.SMEM)]
        + [pl.BlockSpec(memory_space=space) for space in spaces],
        out_specs=[pl.BlockSpec(memory_space=pltpu.VMEM) for _ in outs],
        out_shape=outs,
        scratch_shapes=scratch,
        compiler_params=pltpu.CompilerParams(vmem_limit_bytes=VMEM_LIMIT),
        cost_estimate=pl.CostEstimate(flops=flops, bytes_accessed=0, transcendentals=0),
        name=name,
    )(meta, *operands)


def times(rows, block):
    return jnp.dot(rows, block, preferred_element_type=jnp.float32)


def times_transposed(rows, block):
    return lax.dot_general(
        rows, block, (((1,), (1,)), ((), ())), preferred_element_type=jnp.float32
    )


def add_times(meta, held, place, rows, out):
    @pl.when(meta[place] > 0)
    def _():
        out[...] += times(rows[...], held[place])


def load(chunks, meta, blocks, perturb, innovation, weight, *refs):
    own, outs = refs[:chunks], refs[chunks:2 * chunks]
    held, held_perturb, held_innovation, held_weight, turned, arrived = refs[2 * chunks:]
    slots = held.shape[0]
    copies = [
        pltpu.make_async_copy(blocks.at[0, meta[slots + k]], held.at[k], arrived.at[k])
        for k in range(slots)
    ]
    copies += [
        pltpu.make_async_copy(source, target, arrived.at[slots + k])
        for k, (source, target) in enumerate((
            (perturb, held_perturb), (innovation, held_innovation), (weight, held_weight),
        ))
    ]
    for copy in copies:
        copy.start()
    for out in outs:
        out[...] = jnp.zeros_like(out)
    copies[OWN].wait()
    for rows, out in zip(own, outs):
        add_times(meta, held, OWN, rows, out)
    for k, place in enumerate(TURNED):
        copies[place].wait()

        @pl.when(meta[place] > 0)
        def _(k=k, place=place):
            turned[k] = held[place].T

    for k, copy in enumerate(copies):
        if k not in (OWN, *TURNED):
            copy.wait()


def forward_add(chunk, places, meta, held, before, *refs):
    out = refs[-1]
    out[...] = before[...]
    count = out.shape[0]
    for place, rows in zip(places, refs):
        place = meta[place[0]] if isinstance(place, tuple) else place
        if rows.shape[0] > count:
            rows = rows.at[chunk * count:(chunk + 1) * count]
        add_times(meta, held, place, rows, out)


def forward_far(chunk, meta, held, perturb, before, *refs):
    *swapped, out, sent, total = refs
    levels = out.shape[1]
    at = slice(chunk * levels, (chunk + 1) * levels)
    total[...] = before[...]
    @pl.when(meta[SWAPPED] > 0)
    def _():
        rows = jnp.concatenate([v[...] for v in swapped])
        total[...] += times(rows, held[SWAPPED])

    for t in range(out.shape[0]):
        value = sum(
            perturb[t, m, at].astype(jnp.float32) * total[m * levels:(m + 1) * levels]
            for m in range(perturb.shape[1])
        )
        out[t] = value
        sent[t] = value.astype(sent.dtype)


def back_times(held, turned, place, rows):
    if place in TURNED:
        return times(rows[...], turned[TURNED.index(place)])
    return times_transposed(rows[...], held[place])


def transposed_or_zero(meta, held, turned, place, rows, *outs):
    size = outs[0].shape[0]
    alive = meta[place] > 0

    @pl.when(alive)
    def _():
        value = back_times(held, turned, place, rows)
        for k, out in enumerate(outs):
            out[...] = value[k * size:(k + 1) * size].astype(out.dtype)

    @pl.when(jnp.logical_not(alive))
    def _():
        for out in outs:
            out[...] = jnp.zeros_like(out)


def backward_first(chunk, pieces, meta, turned, perturb, innovation, weight, *refs):
    terms, refs = refs[:-4 - pieces], refs[-4 - pieces:]
    adjoint_in, *swap, direct, part, summed = refs
    slots = len(ORDER)
    count, levels, cells = summed.shape
    width = part.shape[-1]
    at = slice(chunk * levels, (chunk + 1) * levels)
    seen = lax.broadcasted_iota(jnp.int32, (levels, cells), 1) < meta[2 * slots]
    residual = []
    for t in range(count):
        value = sum(term[t].astype(jnp.float32) for term in terms)
        summed[t] = value
        residual.append(weight[at] * jnp.where(seen, value - innovation[t, at], 0.0))
    part[...] = summed[:, :, pl.ds(pl.multiple_of(meta[2 * slots + 1] * width, 128), width)]
    for m in range(perturb.shape[1]):
        value = sum(perturb[t, m, at].astype(jnp.float32) * residual[t] for t in range(count))
        adjoint_in[m * levels:(m + 1) * levels] = value.astype(adjoint_in.dtype)
    transposed_or_zero(meta, None, turned, SWAPPED, adjoint_in, *swap)
    transposed_or_zero(meta, None, turned, LATE, adjoint_in, direct)


def backward_through(meta, turned, adjoint_in, *refs):
    *swap, out = refs
    size = swap[0].shape[0]
    alive = meta[EARLY] > 0

    @pl.when(alive)
    def _():
        value = back_times(None, turned, EARLY, adjoint_in)
        for k, piece in enumerate(swap):
            at = slice(k * size, (k + 1) * size)
            out[at] = (value[at] + piece[...].astype(jnp.float32)).astype(out.dtype)

    @pl.when(jnp.logical_not(alive))
    def _():
        for k, piece in enumerate(swap):
            out[k * size:(k + 1) * size] = piece[...]


def backward_rest(meta, held, adjoint_in, *outs):
    transposed_or_zero(meta, held, None, PARTNER, adjoint_in, *outs[:-1])
    transposed_or_zero(meta, held, None, OWN, adjoint_in, outs[-1])


def backward_one(place, meta, held, adjoint_in, out):
    transposed_or_zero(meta, held, None, place, adjoint_in, out)


def mark(meta, value, kept, out):
    out[...] = kept[...]


def settle(coeffs, *refs):
    *terms, out = refs
    value = coeffs[...].reshape(out.shape)
    if terms[0].shape == out.shape:
        value = value + terms[0][...].astype(jnp.float32)
        terms = terms[1:]
    if terms:
        value = value + jnp.concatenate([v[...].astype(jnp.float32) for v in terms])
    out[...] = value


def finish(chunk, terms, *refs):
    refs, (out, value, sent) = refs[:terms], refs[-3:]
    members, levels, _ = value.shape
    size = members // 2
    copies = []
    for k in range(2):
        rows = slice(k * size * levels, (k + 1) * size * levels)
        some = slice(k * size, (k + 1) * size)
        value[some] = sum(v[rows].astype(jnp.float32) for v in refs).reshape(size, levels, -1)
        copies.append(pltpu.make_async_copy(
            value.at[some], out.at[some, chunk * levels:(chunk + 1) * levels], sent.at[k]
        ))
        copies[k].start()
    for copy in copies:
        copy.wait()


def shards(coeffs, perturb, blocks, neighbours, live, obs_count, innovation, obs_weight):
    members, levels, cells = coeffs.shape
    window = perturb.shape[0]
    slots = blocks.shape[1]
    tile_count = lax.axis_size("tile")
    groups = lax.axis_size("member")
    tile_index = lax.axis_index("tile")
    group_index = lax.axis_index("member")
    half, full = jnp.bfloat16, jnp.float32
    part = levels // CHUNKS
    rows = members * part
    width = cells // groups
    shape = jax.ShapeDtypeStruct
    rows_half, rows_full = shape((rows, cells), half), shape((rows, cells), full)

    side = 1 - 2 * (tile_index % 2)
    radius = (slots - 1) // 2
    offset = (neighbours[0] - tile_index) % tile_count
    offset = jnp.where(offset > radius, offset - tile_count, offset) * side
    match = offset[None, :] == jnp.array(ORDER, jnp.int32)[:, None]
    slot = jnp.sum(jnp.where(match, jnp.arange(slots)[None, :], 0), axis=1)
    places = jnp.where((tile_index // 2) % 2 == 0, jnp.array([LATE, EARLY]), jnp.array([EARLY, LATE]))
    meta = jnp.concatenate(
        [(slot < live[0]).astype(slot.dtype), slot, obs_count, group_index[None], places]
    ).astype(jnp.int32)

    inward = shift_pairs(tile_count, lambda core, chip: -2 if core == 0 else 2)
    outward = shift_pairs(tile_count, lambda core, chip: 2 if core == 0 else -2)
    below = shift_pairs(tile_count, lambda core, chip: -2 if (core + chip) % 2 == 0 else 2)
    above = shift_pairs(tile_count, lambda core, chip: 2 if (core + chip) % 2 == 0 else -2)
    even = (tile_index // 2) % 2 == 0
    across = shift_pairs(tile_count, lambda core, chip: 1 if core == 0 else -1)

    own = []
    for c in range(CHUNKS):
        source = coeffs if c == 0 else after(coeffs, own[c - 1])
        own.append(source[:, c * part:(c + 1) * part].astype(half).reshape(rows, cells))
    distant = [
        pltpu.with_memory_space_constraint(v, pltpu.HBM)
        for v in (blocks, perturb, innovation, obs_weight)
    ]
    *near, held, held_perturb, held_innovation, held_weight, turned = call(
        functools.partial(load, CHUNKS), meta, (*distant, *own),
        [rows_full] * CHUNKS
        + [pltpu.VMEM(v.shape, v.dtype) for v in (blocks[0], perturb, innovation, obs_weight)]
        + [pltpu.VMEM((len(TURNED), cells, cells), half)],
        "load", [pltpu.SemaphoreType.DMA((slots + 3,))],
        [pltpu.HBM] * 4 + [pltpu.VMEM] * CHUNKS,
    )
    held, held_perturb, held_innovation, held_weight, turned = map(
        resident, (held, held_perturb, held_innovation, held_weight, turned)
    )

    def add(c, before, name, **rows):
        places = tuple(PLACES[key] for key in rows)
        [total] = call(
            functools.partial(forward_add, c, places), meta, (held, before, *rows.values()), [rows_full], name
        )
        return total

    def forwarded(pieces, below, above, other):
        below, above, _ = lax.optimization_barrier((below, above, other))
        size = rows // pieces
        cuts = [slice(k * size, (k + 1) * size) for k in range(pieces)]
        return [lax.ppermute(jnp.where(even, above[at], below[at]), "tile", across) for at in cuts]

    def observe(c, total, swapped):
        return call(
            functools.partial(forward_far, c), meta, (held, held_perturb, total, *swapped),
            [shape((window, part, cells), full), shape((window, part, cells), half)],
            "forward_far", [pltpu.VMEM((rows, cells), full)],
        )

    def cut(pieces):
        return [shape((rows // pieces, cells), half)] * pieces

    def respond(c, pieces, terms, weight, *others):
        adjoint_in, *swap, direct, increment = call(
            functools.partial(backward_first, c, pieces), meta,
            (turned, held_perturb, held_innovation, weight, after(terms[0], *others), *terms[1:]),
            [rows_half, *cut(pieces), rows_half, shape((window, part, width), full)],
            "backward_first", [pltpu.VMEM((window, part, cells), full)],
        )
        return adjoint_in, swap, direct, increment

    def add_through(adjoint_in, swap):
        [through] = call(
            backward_through, meta, (turned, adjoint_in, *swap), [rows_half], "backward_through"
        )
        return through

    def arrived(value, kept):
        [kept] = call(
            mark, meta, (value, kept), [pltpu.VMEM(kept.shape, kept.dtype)], "mark",
            spaces=[pl.ANY, pltpu.VMEM], flops=HEAVY,
        )
        return resident(kept)

    def rest(pieces, adjoint_in, *others):
        *second, kept = call(
            backward_rest, meta, (held, after(adjoint_in, *others)), [*cut(pieces), rows_full],
            "backward_rest",
        )
        return second, kept

    def one(place, out, name, adjoint_in, *others):
        [value] = call(
            functools.partial(backward_one, place), meta, (held, after(adjoint_in, *others)), [out], name
        )
        return value

    def settled(c, *terms):
        return pl.pallas_call(
            settle,
            grid=(1,),
            in_specs=[pl.BlockSpec((members, part, cells), lambda i: (0, c, 0))]
            + [pl.BlockSpec(v.shape, lambda i: (0, 0)) for v in terms],
            out_specs=pl.BlockSpec((rows, cells), lambda i: (0, 0)),
            out_shape=rows_full,
            compiler_params=pltpu.CompilerParams(vmem_limit_bytes=VMEM_LIMIT),
            cost_estimate=pl.CostEstimate(flops=0, bytes_accessed=0, transcendentals=0),
            name="settle",
        )(coeffs, *terms)

    def finished(c, gradient, *terms):
        return pl.pallas_call(
            functools.partial(finish, c, len(terms)),
            in_specs=[pl.BlockSpec(memory_space=pltpu.VMEM)] * len(terms)
            + [pl.BlockSpec(memory_space=pl.ANY)] * len(gradient),
            out_specs=pl.BlockSpec(memory_space=pl.ANY),
            out_shape=shape(coeffs.shape, full),
            scratch_shapes=[pltpu.VMEM((members, part, cells), full), pltpu.SemaphoreType.DMA((2,))],
            input_output_aliases={len(terms): 0} if gradient else {},
            compiler_params=pltpu.CompilerParams(vmem_limit_bytes=VMEM_LIMIT),
            cost_estimate=pl.CostEstimate(flops=0, bytes_accessed=0, transcendentals=0),
            name="finish",
        )(*terms, *gradient)

    below0 = lax.ppermute(own[0], "tile", below)
    above0 = lax.ppermute(own[0], "tile", above)
    partner = lax.ppermute(jnp.concatenate(after(own, near[0])), "tile", across)
    swapped0 = forwarded(2, below0, above0, near[0])
    below1 = lax.ppermute(after(own[1], below0, above0), "tile", below)
    above1 = lax.ppermute(after(own[1], below0, above0), "tile", above)
    total0 = add(0, near[0], "forward_mid", partner=partner, below=below0, above=above0)
    increment0, sent0 = observe(0, total0, swapped0)
    terms0 = member_terms(increment0, sent0, groups)
    near1 = add(1, near[1], "forward_near", partner=partner)
    adjoint0, swap0, direct0, part0 = respond(0, 1, terms0, held_weight, near1)
    swap0 = [lax.ppermute(v, "tile", across) for v in swap0]
    direct0 = lax.ppermute(direct0, "tile", inward)
    swapped1 = forwarded(2, below1, above1, adjoint0)
    total1 = add(1, near1, "forward_mid", below=below1, above=above1)
    increment1, sent1 = observe(1, total1, swapped1)
    through0 = add_through(adjoint0, swap0)
    terms1 = member_terms(increment1, sent1, groups)
    through0 = lax.ppermute(through0, "tile", outward)
    adjoint1, swap1, direct1, part1 = respond(1, 2, terms1, arrived(direct0, held_weight))
    swap1 = [lax.ppermute(v, "tile", across) for v in swap1]
    second0 = one(PARTNER, rows_half, "backward_second", adjoint0, *swap1)
    second0 = lax.ppermute(second0, "tile", across)
    direct1 = lax.ppermute(direct1, "tile", inward)
    through1 = lax.ppermute(add_through(adjoint1, swap1), "tile", outward)
    second1, kept1 = rest(2, adjoint1, *swap1, through0)
    second1 = [lax.ppermute(v, "tile", across) for v in second1]
    kept0 = one(OWN, rows_full, "backward_kept", adjoint0, *second1)
    found0 = settled(0, direct0)
    found1 = settled(1, kept1, *second1)
    gradient = finished(0, (), found0, kept0, second0, through0)
    gradient = finished(1, (gradient,), found1, direct1, through1)
    return (jnp.concatenate((part0, part1), axis=1), gradient)


def solution(mesh):
    placed = (
        P("member", None, "tile"),
        P(None, "member", None, "tile"),
        P("tile", None, None, None),
        P("tile", None),
        P("tile"),
        P("tile"),
        P(None, None, "tile"),
        P(None, "tile"),
    )
    return jax.shard_map(
        shards,
        mesh=mesh,
        in_specs=placed,
        out_specs=(P(None, None, ("tile", "member")), P("member", None, "tile")),
        check_vma=False,
    )
```

```python
import functools
import jax
import jax.numpy as jnp
from jax import lax
from jax.experimental import pallas as pl
from jax.experimental.pallas import tpu as pltpu
from jax.sharding import PartitionSpec as P

CHUNKS = 2
HEAVY = 100 * 10**9
VMEM_LIMIT = 20 * 1024 * 1024
OWN, PARTNER, EARLY, SWAPPED, LATE = range(5)
PLACES = {"partner": PARTNER, "below": (12,), "above": (13,)}
ORDER = (0, 1, 2, -1, -2)
TURNED = (SWAPPED, LATE, EARLY)


def shift_pairs(count, step):
    return [(tile, (tile + step(tile % 2, tile // 2)) % count) for tile in range(count)]


def member_terms(value, sent, groups):
    terms, done = [value], 1
    while done < groups:
        if done > 1:
            value = functools.reduce(jnp.add, terms)
            sent = value.astype(sent.dtype)
        masks = (1, 2, 3) if groups // done >= 4 else (1,)
        terms = [value]
        for mask in masks:
            pairs = [(g, g ^ (mask * done)) for g in range(groups)]
            terms.append(lax.ppermute(sent, "member", pairs))
        done *= len(masks) + 1
    return terms


def after(value, *others):
    return lax.optimization_barrier((value, *others))[0]


def resident(value):
    return pltpu.with_memory_space_constraint(value, pltpu.VMEM)


def call(body, meta, operands, outs, name, scratch=(), spaces=None, flops=0):
    spaces = spaces or [pltpu.VMEM] * len(operands)
    return pl.pallas_call(
        body,
        in_specs=[pl.BlockSpec(memory_space=pltpu.SMEM)]
        + [pl.BlockSpec(memory_space=space) for space in spaces],
        out_specs=[pl.BlockSpec(memory_space=pltpu.VMEM) for _ in outs],
        out_shape=outs,
        scratch_shapes=scratch,
        compiler_params=pltpu.CompilerParams(vmem_limit_bytes=VMEM_LIMIT),
        cost_estimate=pl.CostEstimate(flops=flops, bytes_accessed=0, transcendentals=0),
        name=name,
    )(meta, *operands)


def times(rows, block):
    return jnp.dot(rows, block, preferred_element_type=jnp.float32)


def times_transposed(rows, block):
    return lax.dot_general(
        rows, block, (((1,), (1,)), ((), ())), preferred_element_type=jnp.float32
    )


def add_times(meta, held, place, rows, out):
    @pl.when(meta[place] > 0)
    def _():
        out[...] += times(rows[...], held[place])


def load(chunks, meta, blocks, perturb, innovation, weight, *refs):
    own, outs = refs[:chunks], refs[chunks:2 * chunks]
    held, held_perturb, held_innovation, held_weight, turned, arrived = refs[2 * chunks:]
    slots = held.shape[0]
    copies = [
        pltpu.make_async_copy(blocks.at[0, meta[slots + k]], held.at[k], arrived.at[k])
        for k in range(slots)
    ]
    copies += [
        pltpu.make_async_copy(source, target, arrived.at[slots + k])
        for k, (source, target) in enumerate((
            (perturb, held_perturb), (innovation, held_innovation), (weight, held_weight),
        ))
    ]
    for copy in copies:
        copy.start()
    for out in outs:
        out[...] = jnp.zeros_like(out)
    copies[OWN].wait()
    for rows, out in zip(own, outs):
        add_times(meta, held, OWN, rows, out)
    for k, place in enumerate(TURNED):
        copies[place].wait()

        @pl.when(meta[place] > 0)
        def _(k=k, place=place):
            turned[k] = held[place].T

    for k, copy in enumerate(copies):
        if k not in (OWN, *TURNED):
            copy.wait()


def forward_add(chunk, places, meta, held, before, *refs):
    out = refs[-1]
    out[...] = before[...]
    count = out.shape[0]
    for place, rows in zip(places, refs):
        place = meta[place[0]] if isinstance(place, tuple) else place
        if rows.shape[0] > count:
            rows = rows.at[chunk * count:(chunk + 1) * count]
        add_times(meta, held, place, rows, out)


def forward_far(chunk, meta, held, perturb, before, *refs):
    *swapped, out, sent, total = refs
    levels = out.shape[1]
    at = slice(chunk * levels, (chunk + 1) * levels)
    total[...] = before[...]
    @pl.when(meta[SWAPPED] > 0)
    def _():
        rows = jnp.concatenate([v[...] for v in swapped])
        total[...] += times(rows, held[SWAPPED])

    for t in range(out.shape[0]):
        value = sum(
            perturb[t, m, at].astype(jnp.float32) * total[m * levels:(m + 1) * levels]
            for m in range(perturb.shape[1])
        )
        out[t] = value
        sent[t] = value.astype(sent.dtype)


def back_times(held, turned, place, rows):
    if place in TURNED:
        return times(rows[...], turned[TURNED.index(place)])
    return times_transposed(rows[...], held[place])


def transposed_or_zero(meta, held, turned, place, rows, *outs):
    size = outs[0].shape[0]
    alive = meta[place] > 0

    @pl.when(alive)
    def _():
        value = back_times(held, turned, place, rows)
        for k, out in enumerate(outs):
            out[...] = value[k * size:(k + 1) * size].astype(out.dtype)

    @pl.when(jnp.logical_not(alive))
    def _():
        for out in outs:
            out[...] = jnp.zeros_like(out)


def backward_first(chunk, pieces, meta, turned, perturb, innovation, weight, *refs):
    terms, refs = refs[:-4 - pieces], refs[-4 - pieces:]
    adjoint_in, *swap, direct, part, summed = refs
    slots = len(ORDER)
    count, levels, cells = summed.shape
    width = part.shape[-1]
    at = slice(chunk * levels, (chunk + 1) * levels)
    seen = lax.broadcasted_iota(jnp.int32, (levels, cells), 1) < meta[2 * slots]
    residual = []
    for t in range(count):
        value = sum(term[t].astype(jnp.float32) for term in terms)
        summed[t] = value
        residual.append(weight[at] * jnp.where(seen, value - innovation[t, at], 0.0))
    part[...] = summed[:, :, pl.ds(pl.multiple_of(meta[2 * slots + 1] * width, 128), width)]
    for m in range(perturb.shape[1]):
        value = sum(perturb[t, m, at].astype(jnp.float32) * residual[t] for t in range(count))
        adjoint_in[m * levels:(m + 1) * levels] = value.astype(adjoint_in.dtype)
    transposed_or_zero(meta, None, turned, SWAPPED, adjoint_in, *swap)
    transposed_or_zero(meta, None, turned, LATE, adjoint_in, direct)


def backward_through(meta, turned, adjoint_in, *refs):
    *swap, out = refs
    size = swap[0].shape[0]
    alive = meta[EARLY] > 0

    @pl.when(alive)
    def _():
        value = back_times(None, turned, EARLY, adjoint_in)
        for k, piece in enumerate(swap):
            at = slice(k * size, (k + 1) * size)
            out[at] = (value[at] + piece[...].astype(jnp.float32)).astype(out.dtype)

    @pl.when(jnp.logical_not(alive))
    def _():
        for k, piece in enumerate(swap):
            out[k * size:(k + 1) * size] = piece[...]


def backward_rest(meta, held, adjoint_in, *outs):
    transposed_or_zero(meta, held, None, PARTNER, adjoint_in, *outs[:-1])
    transposed_or_zero(meta, held, None, OWN, adjoint_in, outs[-1])


def backward_one(place, meta, held, adjoint_in, out):
    transposed_or_zero(meta, held, None, place, adjoint_in, out)


def settle(coeffs, *refs):
    *terms, out = refs
    value = coeffs[...].reshape(out.shape)
    if terms[0].shape == out.shape:
        value = value + terms[0][...].astype(jnp.float32)
        terms = terms[1:]
    if terms:
        value = value + jnp.concatenate([v[...].astype(jnp.float32) for v in terms])
    out[...] = value


def finish(chunk, terms, *refs):
    refs, (out, value, sent) = refs[:terms], refs[-3:]
    members, levels, _ = value.shape
    size = members // 2
    copies = []
    for k in range(2):
        rows = slice(k * size * levels, (k + 1) * size * levels)
        some = slice(k * size, (k + 1) * size)
        value[some] = sum(v[rows].astype(jnp.float32) for v in refs).reshape(size, levels, -1)
        copies.append(pltpu.make_async_copy(
            value.at[some], out.at[some, chunk * levels:(chunk + 1) * levels], sent.at[k]
        ))
        copies[k].start()
    for copy in copies:
        copy.wait()


def shards(coeffs, perturb, blocks, neighbours, live, obs_count, innovation, obs_weight):
    members, levels, cells = coeffs.shape
    window = perturb.shape[0]
    slots = blocks.shape[1]
    tile_count = lax.axis_size("tile")
    groups = lax.axis_size("member")
    tile_index = lax.axis_index("tile")
    group_index = lax.axis_index("member")
    half, full = jnp.bfloat16, jnp.float32
    part = levels // CHUNKS
    rows = members * part
    width = cells // groups
    shape = jax.ShapeDtypeStruct
    rows_half, rows_full = shape((rows, cells), half), shape((rows, cells), full)

    side = 1 - 2 * (tile_index % 2)
    radius = (slots - 1) // 2
    offset = (neighbours[0] - tile_index) % tile_count
    offset = jnp.where(offset > radius, offset - tile_count, offset) * side
    match = offset[None, :] == jnp.array(ORDER, jnp.int32)[:, None]
    slot = jnp.sum(jnp.where(match, jnp.arange(slots)[None, :], 0), axis=1)
    places = jnp.where((tile_index // 2) % 2 == 0, jnp.array([LATE, EARLY]), jnp.array([EARLY, LATE]))
    meta = jnp.concatenate(
        [(slot < live[0]).astype(slot.dtype), slot, obs_count, group_index[None], places]
    ).astype(jnp.int32)

    inward = shift_pairs(tile_count, lambda core, chip: -2 if core == 0 else 2)
    outward = shift_pairs(tile_count, lambda core, chip: 2 if core == 0 else -2)
    below = shift_pairs(tile_count, lambda core, chip: -2 if (core + chip) % 2 == 0 else 2)
    above = shift_pairs(tile_count, lambda core, chip: 2 if (core + chip) % 2 == 0 else -2)
    even = (tile_index // 2) % 2 == 0
    across = shift_pairs(tile_count, lambda core, chip: 1 if core == 0 else -1)

    own = []
    for c in range(CHUNKS):
        source = coeffs if c == 0 else after(coeffs, own[c - 1])
        own.append(source[:, c * part:(c + 1) * part].astype(half).reshape(rows, cells))
    distant = [
        pltpu.with_memory_space_constraint(v, pltpu.HBM)
        for v in (blocks, perturb, innovation, obs_weight)
    ]
    *near, held, held_perturb, held_innovation, held_weight, turned = call(
        functools.partial(load, CHUNKS), meta, (*distant, *own),
        [rows_full] * CHUNKS
        + [pltpu.VMEM(v.shape, v.dtype) for v in (blocks[0], perturb, innovation, obs_weight)]
        + [pltpu.VMEM((len(TURNED), cells, cells), half)],
        "load", [pltpu.SemaphoreType.DMA((slots + 3,))],
        [pltpu.HBM] * 4 + [pltpu.VMEM] * CHUNKS,
    )
    held, held_perturb, held_innovation, held_weight, turned = map(
        resident, (held, held_perturb, held_innovation, held_weight, turned)
    )

    def add(c, before, name, **rows):
        places = tuple(PLACES[key] for key in rows)
        [total] = call(
            functools.partial(forward_add, c, places), meta, (held, before, *rows.values()), [rows_full], name
        )
        return total

    def forwarded(pieces, below, above, other):
        below, above, _ = lax.optimization_barrier((below, above, other))
        size = rows // pieces
        cuts = [slice(k * size, (k + 1) * size) for k in range(pieces)]
        return [lax.ppermute(jnp.where(even, above[at], below[at]), "tile", across) for at in cuts]

    def observe(c, total, swapped):
        return call(
            functools.partial(forward_far, c), meta, (held, held_perturb, total, *swapped),
            [shape((window, part, cells), full), shape((window, part, cells), half)],
            "forward_far", [pltpu.VMEM((rows, cells), full)],
        )

    def cut(pieces):
        return [shape((rows // pieces, cells), half)] * pieces

    def respond(c, pieces, terms, weight, *others):
        adjoint_in, *swap, direct, increment = call(
            functools.partial(backward_first, c, pieces), meta,
            (turned, held_perturb, held_innovation, weight, after(terms[0], *others), *terms[1:]),
            [rows_half, *cut(pieces), rows_half, shape((window, part, width), full)],
            "backward_first", [pltpu.VMEM((window, part, cells), full)],
        )
        return adjoint_in, swap, direct, increment

    def add_through(adjoint_in, swap):
        [through] = call(
            backward_through, meta, (turned, adjoint_in, *swap), [rows_half], "backward_through"
        )
        return through

    def rest(pieces, adjoint_in, *others):
        *second, kept = call(
            backward_rest, meta, (held, after(adjoint_in, *others)), [*cut(pieces), rows_full],
            "backward_rest",
        )
        return second, kept

    def one(place, out, name, adjoint_in, *others, flops=0):
        [value] = call(
            functools.partial(backward_one, place), meta, (held, after(adjoint_in, *others)), [out], name,
            flops=flops,
        )
        return value

    def settled(c, *terms):
        return pl.pallas_call(
            settle,
            grid=(1,),
            in_specs=[pl.BlockSpec((members, part, cells), lambda i: (0, c, 0))]
            + [pl.BlockSpec(v.shape, lambda i: (0, 0)) for v in terms],
            out_specs=pl.BlockSpec((rows, cells), lambda i: (0, 0)),
            out_shape=rows_full,
            compiler_params=pltpu.CompilerParams(vmem_limit_bytes=VMEM_LIMIT),
            cost_estimate=pl.CostEstimate(flops=0, bytes_accessed=0, transcendentals=0),
            name="settle",
        )(coeffs, *terms)

    def finished(c, gradient, *terms):
        return pl.pallas_call(
            functools.partial(finish, c, len(terms)),
            in_specs=[pl.BlockSpec(memory_space=pltpu.VMEM)] * len(terms)
            + [pl.BlockSpec(memory_space=pl.ANY)] * len(gradient),
            out_specs=pl.BlockSpec(memory_space=pl.ANY),
            out_shape=shape(coeffs.shape, full),
            scratch_shapes=[pltpu.VMEM((members, part, cells), full), pltpu.SemaphoreType.DMA((2,))],
            input_output_aliases={len(terms): 0} if gradient else {},
            compiler_params=pltpu.CompilerParams(vmem_limit_bytes=VMEM_LIMIT),
            cost_estimate=pl.CostEstimate(flops=0, bytes_accessed=0, transcendentals=0),
            name="finish",
        )(*terms, *gradient)

    below0 = lax.ppermute(own[0], "tile", below)
    above0 = lax.ppermute(own[0], "tile", above)
    partner = lax.ppermute(jnp.concatenate(after(own, near[0])), "tile", across)
    swapped0 = forwarded(2, below0, above0, near[0])
    below1 = lax.ppermute(after(own[1], below0, above0), "tile", below)
    above1 = lax.ppermute(after(own[1], below0, above0), "tile", above)
    total0 = add(0, near[0], "forward_mid", partner=partner, below=below0, above=above0)
    increment0, sent0 = observe(0, total0, swapped0)
    terms0 = member_terms(increment0, sent0, groups)
    near1 = add(1, near[1], "forward_near", partner=partner)
    adjoint0, swap0, direct0, part0 = respond(0, 1, terms0, held_weight, near1)
    swap0 = [lax.ppermute(v, "tile", across) for v in swap0]
    direct0 = lax.ppermute(direct0, "tile", inward)
    swapped1 = forwarded(2, below1, above1, adjoint0)
    total1 = add(1, near1, "forward_mid", below=below1, above=above1)
    increment1, sent1 = observe(1, total1, swapped1)
    through0 = add_through(adjoint0, swap0)
    terms1 = member_terms(increment1, sent1, groups)
    through0 = lax.ppermute(through0, "tile", outward)
    second0 = one(PARTNER, rows_half, "backward_second", adjoint0, direct0, flops=HEAVY)
    adjoint1, swap1, direct1, part1 = respond(1, 2, terms1, held_weight, second0)
    swap1 = [lax.ppermute(v, "tile", across) for v in swap1]
    second0 = lax.ppermute(second0, "tile", across)
    direct1 = lax.ppermute(direct1, "tile", inward)
    through1 = lax.ppermute(add_through(adjoint1, swap1), "tile", outward)
    second1, kept1 = rest(2, adjoint1, *swap1, through0)
    second1 = [lax.ppermute(v, "tile", across) for v in second1]
    kept0 = one(OWN, rows_full, "backward_kept", adjoint0, *second1)
    found0 = settled(0, direct0)
    found1 = settled(1, kept1, *second1)
    gradient = finished(0, (), found0, kept0, second0, through0)
    gradient = finished(1, (gradient,), found1, direct1, through1)
    return (jnp.concatenate((part0, part1), axis=1), gradient)


def solution(mesh):
    placed = (
        P("member", None, "tile"),
        P(None, "member", None, "tile"),
        P("tile", None, None, None),
        P("tile", None),
        P("tile"),
        P("tile"),
        P(None, None, "tile"),
        P(None, "tile"),
    )
    return jax.shard_map(
        shards,
        mesh=mesh,
        in_specs=placed,
        out_specs=(P(None, None, ("tile", "member")), P("member", None, "tile")),
        check_vma=False,
    )
```
